512 devices in a mesh: inner: 8 (over y, x_hi), outer: 32 (over z, core), head: 2 (over x_lo).
Axes of the slice: x: 4 (x_hi: 2, x_lo: 2; x = x_hi * 2 + x_lo), y: 4, z: 16, core: 2. Of those that a mesh axis runs over, the one named last changes fastest.
Arguments:
- queries: bfloat16 [65536, 2048], P(('inner', 'outer'), 'head'), may hold values from -6 to 6
- keys: bfloat16 [65536, 512], P(('inner', 'outer')), may hold values from -6 to 6
- values: bfloat16 [65536, 512], P(('inner', 'outer')), may hold values from -6 to 6
- attn_out: bfloat16 [65536, 2048], P(('inner', 'outer'), 'head'), may hold values from -6 to 6
- grad_out: bfloat16 [65536, 2048], P(('inner', 'outer'), 'head'), may hold values from -96 to 96
- row_total: float32 [16, 65536], P('head', ('inner', 'outer')), may hold values from 2048 to 8192
- block_ids: int32 [512], replicated, may hold values from 0 to 511, each once
Outputs:
- grad_queries: bfloat16 [65536, 2048], P(('inner', 'outer'), 'head')
- grad_keys: bfloat16 [65536, 512], P(('inner', 'outer'), 'head')
- grad_values: bfloat16 [65536, 512], P(('inner', 'outer'), 'head')
The draws below stay inside these ranges and needn't reach their ends.
Inputs may be any that keep to these rules, and one draw needn't show every extreme that they name: `block_ids`: A permutation: every sequence block is stored exactly once.
All inputs are finite; a program needn't handle non-finite values.
Results may differ from the reference program's by a relative error of at most 0.005.
Values may be sent and summed in bfloat16 or wider, within the bound.
No kernel may reach another device: no remote copies, remote signals or barrier semaphores. Data moves between devices by JAX's collectives and lax.ppermute only.
A program may use at most 64 MiB of HBM per device.

```python
import math
import jax
import jax.numpy as jnp
from jax import lax

QH = 16
KVH = 4
HD = 128
TOK = 256
B = 128
CYCLE = 8
GROUPS = 32
BLOCKS = 512
SEQ = 65536


def block_levels(rng, dims, pieces, low, high):
    def one(dim, blocks):
        draws = jax.random.uniform(jax.random.fold_in(jax.random.fold_in(rng, 6), dim), (blocks,), jnp.float32, low / len(pieces), high / len(pieces))
        return jnp.repeat(jnp.exp(draws), dims[dim] // blocks).reshape((-1,) + (1,) * (len(dims) - dim - 1))

    gain = one(*pieces[0])
    for cut in pieces[1:]:
        gain = gain * one(*cut)
    return gain


def normal_values(key, shape, deviation, limit, pieces=(), held_as=jnp.bfloat16):
    values = jax.random.normal(key, shape, jnp.float32) * deviation
    if len(pieces) > 0:
        values = block_levels(key, shape, pieces, -0.22, 0.18) * values
    return jnp.clip(values, min=-limit, max=limit).astype(held_as)


def setup_inputs(seed: int = 0) -> dict:
    streams_of = jax.random.split(jax.random.key(seed), 8)
    queries = normal_values(streams_of[0], (SEQ, QH * HD), 1.0, 6.0, ((0, 256), (1, 2)))
    keys = normal_values(streams_of[1], (SEQ, KVH * HD), 1.0, 6.0, ((0, 256),))
    values = normal_values(streams_of[2], (SEQ, KVH * HD), 1.0, 6.0, ((0, 256),))
    attn_out = normal_values(streams_of[3], (SEQ, QH * HD), 1.0, 6.0, ((0, 256), (1, 2)))
    grad_out = normal_values(streams_of[4], (SEQ, QH * HD), 16.0, 96.0, ((0, 256), (1, 2)))
    row_total = jnp.clip(jnp.exp(math.log(8192.0) - 1.3862944 * jax.random.uniform(streams_of[5], (QH, SEQ), jnp.float32) ** block_levels(streams_of[5], (QH, SEQ), ((0, 2), (1, 256)), -0.2, 0.2)), 2048.0, 8192.0)
    block_ids = jax.random.permutation(streams_of[6], BLOCKS).astype(jnp.int32)
    return dict(queries=queries, keys=keys, values=values, attn_out=attn_out, grad_out=grad_out, row_total=row_total, block_ids=block_ids)


def head_grads(query_one, grad_one, delta_one, logt_one, key_one, value_one, visible, scale):
    query_f = query_one.astype(jnp.float32)
    grad_f = grad_one.astype(jnp.float32)
    key_f = key_one.astype(jnp.float32)
    value_f = value_one.astype(jnp.float32)
    scores = jnp.einsum('qmd,kd->mqk', query_f, key_f) * scale
    prob = jnp.where(visible[None], jnp.exp(scores - logt_one[:, :, None]), jnp.float32(0.0))
    dprob = jnp.einsum('qmd,kd->mqk', grad_f, value_f)
    dscore = prob * (dprob - delta_one[:, :, None])
    prob_low = lax.optimization_barrier(prob.astype(jnp.bfloat16)).astype(jnp.float32)
    dscore_low = lax.optimization_barrier(dscore.astype(jnp.bfloat16)).astype(jnp.float32)
    grad_q = jnp.einsum('mqk,kd->qmd', dscore_low, key_f) * scale
    grad_k = jnp.einsum('mqk,qmd->kd', dscore_low, query_f) * scale
    grad_v = jnp.einsum('mqk,qmd->kd', prob_low, grad_f)
    return (grad_q, grad_k, grad_v)

def reference(queries, keys, values, attn_out, grad_out, row_total, block_ids):
    scale = 1.0 / math.sqrt(HD)
    per_kv = QH // KVH
    length = CYCLE * TOK
    query_all = queries.reshape(CYCLE, GROUPS, TOK, per_kv, KVH, HD)
    grad_all = grad_out.reshape(CYCLE, GROUPS, TOK, per_kv, KVH, HD)
    out_all = attn_out.reshape(CYCLE, GROUPS, TOK, per_kv, KVH, HD)
    delta_all = lax.optimization_barrier(jnp.sum(grad_all.astype(jnp.float32) * out_all.astype(jnp.float32), axis=-1))
    logt_all = jnp.log(row_total).reshape(per_kv, KVH, CYCLE, GROUPS, TOK)
    key_all = keys.reshape(CYCLE, GROUPS, TOK, KVH, HD)
    value_all = values.reshape(CYCLE, GROUPS, TOK, KVH, HD)
    blocks_all = jnp.repeat(block_ids, B).reshape(CYCLE, GROUPS, TOK)

    def per_group(group):
        source = jnp.mod(group - 1, GROUPS).astype(jnp.int32)
        query_g = lax.dynamic_index_in_dim(query_all, group, 1, keepdims=False).reshape(length, per_kv, KVH, HD)
        grad_g = lax.dynamic_index_in_dim(grad_all, group, 1, keepdims=False).reshape(length, per_kv, KVH, HD)
        delta_g = lax.dynamic_index_in_dim(delta_all, group, 1, keepdims=False).reshape(length, per_kv, KVH)
        logt_g = lax.dynamic_index_in_dim(logt_all, group, 3, keepdims=False).reshape(per_kv, KVH, length)
        key_g = lax.dynamic_index_in_dim(key_all, source, 1, keepdims=False).reshape(length, KVH, HD)
        value_g = lax.dynamic_index_in_dim(value_all, source, 1, keepdims=False).reshape(length, KVH, HD)
        query_blocks = lax.dynamic_index_in_dim(blocks_all, group, 1, keepdims=False).reshape(length)
        key_blocks = lax.dynamic_index_in_dim(blocks_all, source, 1, keepdims=False).reshape(length)
        visible = key_blocks[None, :] < query_blocks[:, None]

        def one_head(items):
            query_one, grad_one, delta_one, logt_one, key_one, value_one = items
            return head_grads(query_one, grad_one, delta_one, logt_one, key_one, value_one, visible, scale)
        items = (jnp.moveaxis(query_g, 2, 0), jnp.moveaxis(grad_g, 2, 0), jnp.transpose(delta_g, (2, 1, 0)), jnp.moveaxis(logt_g, 1, 0), jnp.moveaxis(key_g, 1, 0), jnp.moveaxis(value_g, 1, 0))
        return lax.map(one_head, items)
    grad_q, grad_k, grad_v = lax.map(per_group, jnp.arange(GROUPS, dtype=jnp.int32))
    grad_k = jnp.roll(grad_k, -1, axis=0)
    grad_v = jnp.roll(grad_v, -1, axis=0)
    grad_q = grad_q.reshape(GROUPS, KVH, CYCLE, TOK, per_kv, HD)
    grad_q = jnp.transpose(grad_q, (2, 0, 3, 4, 1, 5)).reshape(SEQ, QH * HD)
    grad_k = jnp.transpose(grad_k.reshape(GROUPS, KVH, CYCLE, TOK, HD), (2, 0, 3, 1, 4)).reshape(SEQ, KVH * HD)
    grad_v = jnp.transpose(grad_v.reshape(GROUPS, KVH, CYCLE, TOK, HD), (2, 0, 3, 1, 4)).reshape(SEQ, KVH * HD)
    return (grad_q.astype(jnp.bfloat16), grad_k.astype(jnp.bfloat16), grad_v.astype(jnp.bfloat16))
```

```python
import math

import jax
import jax.numpy as jnp
from jax import lax
from jax.experimental import pallas as pl
from jax.experimental.pallas import tpu as pltpu
from jax.sharding import Mesh
from jax.sharding import PartitionSpec as P

KVH = 4
HD = 128
TOK = 256
HALF = 128
SCALE = 1.0 / math.sqrt(HD)
EXP2_SCALE = SCALE * math.log2(math.e)
HIDDEN = 1.0e30
ROWS = 2 * TOK
AUX = 32
NT = (((1,), (1,)), ((), ()))
NN = (((1,), (0,)), ((), ()))
VMEM = pl.BlockSpec(memory_space=pltpu.VMEM)
SMEM = pl.BlockSpec(memory_space=pltpu.SMEM)
f32 = jnp.float32
bf16 = jnp.bfloat16
PARAMS = pltpu.CompilerParams(vmem_limit_bytes=40 * 2**20)


def dot(a, b, dims):
    return lax.dot_general(a, b, dims, preferred_element_type=f32)


def split3(x):
    a = x.astype(bf16)
    r = x - a.astype(f32)
    b = r.astype(bf16)
    c = (r - b.astype(f32)).astype(bf16)
    return a, b, c


def head_of(x):
    return 2 * (x % 2) + x // 2


def pack_kv(where, keys, values, own, other):
    mine = 2 * where[3] + where[1]
    opposite = 2 * (1 - where[3]) + (1 - where[1])
    for head, out in ((mine, own), (opposite, other)):
        columns = pl.ds(pl.multiple_of(head * HD, HD), HD)
        out[0] = keys[:, columns]
        out[1] = values[:, columns]


def pack_queries(queries, attn_out, grad_out, row_total, message):
    log_total = jnp.log(row_total[...]) * f32(math.log2(math.e))
    ones = jnp.ones((8, HD), bf16)
    for x in range(4):
        head = head_of(x)
        parts = []
        for n in range(2):
            h = n * KVH + head
            columns = slice(h * HD, (h + 1) * HD)
            grad = grad_out[:, columns]
            product = grad.astype(f32) * attn_out[:, columns].astype(f32)
            high = product.astype(bf16)
            low = (product - high.astype(f32)).astype(bf16)
            delta = (dot(ones, high, NT) + dot(ones, low, NT))[0:1]
            parts.append((log_total[h : h + 1], delta))
            for half in range(2):
                rows = slice(half * HALF, (half + 1) * HALF)
                at = (half * 2 + n) * HALF
                message[x, at : at + HALF] = queries[rows, columns]
                message[x, ROWS + at : ROWS + at + HALF] = grad[rows]
        table = []
        for which in range(2):
            for half in range(2):
                for n in range(2):
                    table.append(parts[n][which][:, half * HALF : (half + 1) * HALF])
        table = jnp.concatenate(table, axis=0)
        a, b, c = split3(table)
        pad = jnp.zeros((8, HALF), bf16)
        message[x, 2 * ROWS : 2 * ROWS + AUX] = jnp.concatenate([a, b, c, pad], axis=0)


def attend(ids, message, kv, dq, dkv, dqt, aux):
    for x in range(4):
        table = message[x, 2 * ROWS : 2 * ROWS + AUX, :].astype(f32)
        aux[x] = table[0:8] + table[8:16] + table[16:24]
    dqt[...] = jnp.zeros_like(dqt)

    def row(x, which, half):
        at = which * 4 + half * 2
        return jnp.concatenate([aux[x, at : at + 1, :], aux[x, at + 1 : at + 2, :]], axis=1)

    def shard(j, carry):
        k = kv[j, 0]
        v = kv[j, 1]
        kt = k.T
        dk = jnp.zeros((TOK, HD), f32)
        dv = jnp.zeros((TOK, HD), f32)
        for x_hi in range(2):
            for half in range(2):
                query_block = ids[x_hi * 2 + half]
                hide = [
                    jnp.where(ids[4 + 2 * j + i] < query_block, 0.0, HIDDEN).astype(f32)
                    for i in range(2)
                ]
                for x_lo in range(2):
                    x = x_hi * 2 + x_lo
                    at = half * TOK
                    q = message[x, at : at + TOK, :]
                    g = message[x, ROWS + at : ROWS + at + TOK, :]
                    scores = dot(k, q, NT)
                    dprob = dot(v, g, NT)
                    shift = row(x, 0, half)
                    delta = row(x, 1, half)
                    prob = jnp.concatenate(
                        [
                            jnp.exp2(scores[:HALF] * EXP2_SCALE - (shift + hide[0])),
                            jnp.exp2(scores[HALF:] * EXP2_SCALE - (shift + hide[1])),
                        ],
                        axis=0,
                    )
                    ds = (prob * (dprob - delta)).astype(bf16)
                    dv = dv + dot(prob.astype(bf16), g, NN)
                    dk = dk + dot(ds, q, NN)
                    at = (x * 2 + half) * TOK
                    dqt[:, at : at + TOK] += dot(kt, ds, NN)
        dkv[j, 0] = (dk * SCALE).astype(bf16)
        dkv[j, 1] = dv.astype(bf16)
        return carry

    lax.fori_loop(0, kv.shape[0], shard, 0)
    for x in range(4):
        for half in range(2):
            at = (x * 2 + half) * TOK
            dq[x, half * TOK : (half + 1) * TOK, :] = (dqt[:, at : at + TOK] * SCALE).T.astype(bf16)


def add_partials(parts, own, other):
    for j, out in ((0, own), (1, other)):
        for i in range(2):
            total = parts[0, j, i].astype(f32)
            for y in range(1, parts.shape[0]):
                total = total + parts[y, j, i].astype(f32)
            out[i] = total.astype(bf16)


def unpack(where, dq, own, other, grad_queries, grad_keys, grad_values):
    for x in range(4):
        for n in range(2):
            h = n * KVH + head_of(x)
            for half in range(2):
                at = (half * 2 + n) * HALF
                grad_queries[half * HALF : (half + 1) * HALF, h * HD : (h + 1) * HD] = dq[x, at : at + HALF, :]
    mine = pl.ds(pl.multiple_of(where[1] * HD, HD), HD)
    rest = pl.ds(pl.multiple_of((1 - where[1]) * HD, HD), HD)
    for i, out in ((0, grad_keys), (1, grad_values)):
        out[:, mine] = own[i]
        out[:, rest] = other[i]


def shape(*dims):
    return jax.ShapeDtypeStruct(dims, bf16)


def per_device(queries, keys, values, attn_out, grad_out, row_total, block_ids):
    y_count = lax.axis_size("y")
    outer = lax.axis_size("outer")
    y = lax.axis_index("y")
    x_hi = lax.axis_index("x_hi")
    o = lax.axis_index("outer")
    x_lo = lax.axis_index("x_lo")
    where = jnp.stack([y, x_hi, o, x_lo]).astype(jnp.int32)
    names = ("x_hi", "outer", "x_lo")

    def route(step, turn):
        pairs = []
        for a in range(2):
            for b in range(outer):
                for c in range(2):
                    to_a, to_c = turn(a, c)
                    pairs.append(((a * outer + b) * 2 + c, (to_a * outer + (b + step) % outer) * 2 + to_c))
        return pairs

    own, other = pl.pallas_call(
        pack_kv,
        out_shape=(shape(2, TOK, HD), shape(2, TOK, HD)),
        in_specs=[SMEM, VMEM, VMEM],
        out_specs=(VMEM, VMEM),
        compiler_params=PARAMS,
        name="pack_kv",
    )(where, keys, values)
    own = lax.ppermute(own, names, route(1, lambda a, c: (a, c)))
    other = lax.ppermute(other, names, route(1, lambda a, c: (1 - a, 1 - c)))

    message = pl.pallas_call(
        pack_queries,
        out_shape=shape(4, 2 * ROWS + AUX, HD),
        in_specs=[VMEM] * 4,
        out_specs=VMEM,
        compiler_params=PARAMS,
        name="pack_queries",
    )(queries, attn_out, grad_out, row_total)
    message = lax.all_to_all(message, ("x_hi", "x_lo"), 0, 0, tiled=True)

    kv = lax.all_gather(jnp.stack([own, other]), "y", axis=0, tiled=True)

    stored = block_ids.reshape(y_count, 2, outer, 2)
    query_ids = lax.dynamic_slice(stored, (y, 0, o, 0), (1, 2, 1, 2)).reshape(4)
    key_ids = lax.dynamic_slice(stored, (0, 0, (o - 1) % outer, 0), (y_count, 2, 1, 2)).reshape(y_count, 2, 2)
    key_ids = jnp.where(x_hi == 0, key_ids, key_ids[:, ::-1]).reshape(-1)
    ids = jnp.concatenate([query_ids, key_ids])

    dq, dkv = pl.pallas_call(
        attend,
        out_shape=(shape(4, ROWS, HD), shape(2 * y_count, 2, TOK, HD)),
        in_specs=[SMEM, VMEM, VMEM],
        out_specs=(VMEM, VMEM),
        scratch_shapes=[pltpu.VMEM((HD, 4 * ROWS), f32), pltpu.VMEM((4, 8, HALF), f32)],
        compiler_params=PARAMS,
        name="attend",
    )(ids, message, kv)

    parts = lax.all_to_all(dkv.reshape(y_count, 2, 2, TOK, HD), "y", 0, 0, tiled=True)
    dq = lax.all_to_all(dq, ("x_hi", "x_lo"), 0, 0, tiled=True)
    own, other = pl.pallas_call(
        add_partials,
        out_shape=(shape(2, TOK, HD), shape(2, TOK, HD)),
        in_specs=[VMEM],
        out_specs=(VMEM, VMEM),
        compiler_params=PARAMS,
        name="add_partials",
    )(parts)
    own = lax.ppermute(own, names, route(-1, lambda a, c: (a, c)))
    other = lax.ppermute(other, names, route(-1, lambda a, c: (1 - a, c)))
    return pl.pallas_call(
        unpack,
        out_shape=(shape(TOK, 2 * KVH * HD), shape(TOK, 2 * HD), shape(TOK, 2 * HD)),
        in_specs=[SMEM, VMEM, VMEM, VMEM],
        out_specs=(VMEM, VMEM, VMEM),
        compiler_params=PARAMS,
        name="unpack",
    )(where, dq, own, other)


def solution(mesh):
    inner, outer, head = (mesh.shape[name] for name in ("inner", "outer", "head"))
    fine = Mesh(mesh.devices.reshape(inner // 2, 2, outer, head), ("y", "x_hi", "outer", "x_lo"))
    rows = ("y", "x_hi", "outer")
    in_specs = (
        P(rows, "x_lo"),
        P(rows, None),
        P(rows, None),
        P(rows, "x_lo"),
        P(rows, "x_lo"),
        P("x_lo", rows),
        P(),
    )
    out_specs = (P(rows, "x_lo"), P(rows, "x_lo"), P(rows, "x_lo"))
    return jax.shard_map(per_device, mesh=fine, in_specs=in_specs, out_specs=out_specs, check_vma=False)
```

```python
import functools
import math

import jax
import jax.numpy as jnp
from jax import lax
from jax.experimental import pallas as pl
from jax.experimental.pallas import tpu as pltpu
from jax.sharding import Mesh
from jax.sharding import PartitionSpec as P

KVH = 4
HD = 128
TOK = 256
HALF = 128
SCALE = 1.0 / math.sqrt(HD)
EXP2_SCALE = SCALE * math.log2(math.e)
HIDDEN = 1.0e30
ROWS = 2 * TOK
AUX = 32
NT = (((1,), (1,)), ((), ()))
NN = (((1,), (0,)), ((), ()))
VMEM = pl.BlockSpec(memory_space=pltpu.VMEM)
HBM = pl.BlockSpec(memory_space=pltpu.HBM)
SMEM = pl.BlockSpec(memory_space=pltpu.SMEM)
f32 = jnp.float32
bf16 = jnp.bfloat16
FREE = pl.CostEstimate(flops=0, bytes_accessed=0, transcendentals=0)
PARAMS = pltpu.CompilerParams(vmem_limit_bytes=24 * 2**20)


def dot(a, b, dims):
    return lax.dot_general(a, b, dims, preferred_element_type=f32)


def split3(x):
    a = x.astype(bf16)
    r = x - a.astype(f32)
    b = r.astype(bf16)
    c = (r - b.astype(f32)).astype(bf16)
    return a, b, c


def head_of(x):
    return 2 * (x % 2) + x // 2


def pack_kv(where, keys, values, own, other, sems):
    mine = 2 * where[3] + where[1]
    opposite = 2 * (1 - where[3]) + (1 - where[1])
    copies = []
    for head, out in ((mine, own), (opposite, other)):
        columns = pl.ds(pl.multiple_of(head * HD, HD), HD)
        for i, source in ((0, keys), (1, values)):
            copies.append(pltpu.make_async_copy(source.at[:, columns], out.at[i], sems.at[len(copies)]))
    for copy in copies:
        copy.start()
    for copy in copies:
        copy.wait()


def pack_queries(queries, attn_out, grad_out, row_total, message, q_in, o_in, g_in, t_in, sems):
    copies = [
        pltpu.make_async_copy(source, target, sems.at[i])
        for i, (source, target) in enumerate(((row_total, t_in), (grad_out, g_in), (attn_out, o_in), (queries, q_in)))
    ]
    for copy in copies:
        copy.start()
    ones = jnp.ones((8, HD), bf16)
    copies[0].wait()
    log_total = jnp.log(t_in[...]) * f32(math.log2(math.e))
    copies[1].wait()
    copies[2].wait()
    for x in range(4):
        parts = []
        for n in range(2):
            h = n * KVH + head_of(x)
            columns = slice(h * HD, (h + 1) * HD)
            grad = g_in[:, columns]
            product = grad.astype(f32) * o_in[:, columns].astype(f32)
            high = product.astype(bf16)
            low = (product - high.astype(f32)).astype(bf16)
            delta = (dot(ones, high, NT) + dot(ones, low, NT))[0:1]
            parts.append((log_total[h : h + 1], delta))
            for half in range(2):
                at = ROWS + (half * 2 + n) * HALF
                message[x, at : at + HALF] = grad[half * HALF : (half + 1) * HALF]
        table = []
        for which in range(2):
            for half in range(2):
                for n in range(2):
                    table.append(parts[n][which][:, half * HALF : (half + 1) * HALF])
        table = jnp.concatenate(table, axis=0)
        a, b, c = split3(table)
        pad = jnp.zeros((8, HALF), bf16)
        message[x, 2 * ROWS : 2 * ROWS + AUX] = jnp.concatenate([a, b, c, pad], axis=0)
    copies[3].wait()
    for x in range(4):
        for n in range(2):
            h = n * KVH + head_of(x)
            for half in range(2):
                at = (half * 2 + n) * HALF
                message[x, at : at + HALF] = q_in[half * HALF : (half + 1) * HALF, h * HD : (h + 1) * HD]


def attend(first, last, turn, *refs):
    if first:
        where, ids, message, kv, dq_out, dkv = refs
    else:
        where, ids, message, kv, dq_in, dq_out, dkv = refs
    y, x_hi, o, outer = where[0], where[1], where[2], where[4]
    key_y = (y - turn) & 3
    key_o = jnp.where(o == 0, outer - 1, o - 1)
    k = kv[:, 0].reshape(2 * TOK, HD)
    v = kv[:, 1].reshape(2 * TOK, HD)
    kt = k.T
    key_blocks = []
    for j in range(2):
        key_x = x_hi if j == 0 else 1 - x_hi
        for half in range(2):
            key_blocks.append(ids[((key_y * 2 + key_x) * outer + key_o) * 2 + half])
    dk = jnp.zeros((2 * TOK, HD), f32)
    dv = jnp.zeros((2 * TOK, HD), f32)
    for x in range(4):
        table = message[x, 2 * ROWS : 2 * ROWS + AUX, :].astype(f32)
        table = table[0:8] + table[8:16] + table[16:24]
        shift = jnp.concatenate([table[i : i + 1] for i in range(4)], axis=1)
        delta = jnp.concatenate([table[i : i + 1] for i in range(4, 8)], axis=1)
        query_blocks = [ids[((y * 2 + x // 2) * outer + o) * 2 + half] for half in range(2)]
        q = message[x, 0:ROWS, :]
        g = message[x, ROWS : 2 * ROWS, :]
        scores = dot(k, q, NT)
        dprob = dot(v, g, NT)
        prob = []
        for i in range(4):
            hide = [
                jnp.full((1, TOK), jnp.where(key_blocks[i] < query_blocks[half], 0.0, HIDDEN).astype(f32))
                for half in range(2)
            ]
            row = shift + jnp.concatenate(hide, axis=1)
            prob.append(jnp.exp2(scores[i * HALF : (i + 1) * HALF] * EXP2_SCALE - row))
        prob = jnp.concatenate(prob, axis=0)
        ds = (prob * (dprob - delta)).astype(bf16)
        dv = dv + dot(prob.astype(bf16), g, NN)
        dk = dk + dot(ds, q, NN)
        at = x * ROWS
        dq = dot(kt, ds, NN)
        if not first:
            dq = dq + dq_in[:, at : at + ROWS]
        if last:
            dq_out[x] = (dq * SCALE).T.astype(bf16)
        else:
            dq_out[:, at : at + ROWS] = dq
    dkv[:, 0] = (dk * SCALE).astype(bf16).reshape(2, TOK, HD)
    dkv[:, 1] = dv.astype(bf16).reshape(2, TOK, HD)


def add_partials(a, b, c, d, own, other):
    for j, out in ((0, own), (1, other)):
        for i in range(2):
            total = a[j, i].astype(f32) + b[j, i].astype(f32)
            total = total + (c[j, i].astype(f32) + d[j, i].astype(f32))
            out[i] = total.astype(bf16)


def unpack_queries(dq, grad_queries):
    for x in range(4):
        for n in range(2):
            h = n * KVH + head_of(x)
            for half in range(2):
                at = (half * 2 + n) * HALF
                grad_queries[half * HALF : (half + 1) * HALF, h * HD : (h + 1) * HD] = dq[x, at : at + HALF, :]


def unpack_kv(where, own, other, grad_keys, grad_values, sems):
    mine = pl.ds(pl.multiple_of(where[1] * HD, HD), HD)
    rest = pl.ds(pl.multiple_of((1 - where[1]) * HD, HD), HD)
    copies = []
    for i, out in ((0, grad_keys), (1, grad_values)):
        for columns, part in ((mine, own), (rest, other)):
            copies.append(pltpu.make_async_copy(part.at[i], out.at[:, columns], sems.at[len(copies)]))
    for copy in copies:
        copy.start()
    for copy in copies:
        copy.wait()


def shape(*dims):
    return jax.ShapeDtypeStruct(dims, bf16)


def per_device(queries, keys, values, attn_out, grad_out, row_total, block_ids):
    y_count = lax.axis_size("y")
    outer = lax.axis_size("outer")
    y = lax.axis_index("y")
    x_hi = lax.axis_index("x_hi")
    o = lax.axis_index("outer")
    x_lo = lax.axis_index("x_lo")
    where = jnp.stack([y, x_hi, o, x_lo, jnp.int32(outer)]).astype(jnp.int32)
    names = ("x_hi", "outer", "x_lo")

    def route(step, turn):
        pairs = []
        for a in range(2):
            for b in range(outer):
                for c in range(2):
                    to_a, to_c = turn(a, c)
                    pairs.append(((a * outer + b) * 2 + c, (to_a * outer + (b + step) % outer) * 2 + to_c))
        return pairs

    def along_y(block, turn):
        return lax.ppermute(block, "y", [(i, (i + turn) % y_count) for i in range(y_count)])

    own, other = pl.pallas_call(
        pack_kv,
        out_shape=(shape(2, TOK, HD), shape(2, TOK, HD)),
        in_specs=[SMEM, HBM, HBM],
        out_specs=(VMEM, VMEM),
        scratch_shapes=[pltpu.SemaphoreType.DMA((4,))],
        compiler_params=PARAMS,
        name="pack_kv",
    )(where, keys, values)
    own = lax.ppermute(own, names, route(1, lambda a, c: (a, c)))
    other = lax.ppermute(other, names, route(1, lambda a, c: (1 - a, 1 - c)))

    message = pl.pallas_call(
        pack_queries,
        out_shape=shape(4, 2 * ROWS + AUX, HD),
        in_specs=[HBM] * 4,
        out_specs=VMEM,
        scratch_shapes=[pltpu.VMEM((TOK, 2 * KVH * HD), bf16)] * 3
        + [pltpu.VMEM((2 * KVH, TOK), f32), pltpu.SemaphoreType.DMA((4,))],
        compiler_params=PARAMS,
        name="pack_queries",
    )(queries, attn_out, grad_out, row_total)
    own, other, message = lax.optimization_barrier((own, other, message))
    message = lax.all_to_all(message, ("x_hi", "x_lo"), 0, 0, tiled=True)

    kv = jnp.stack([own, other])
    order = (1, 3, 2, 0)
    blocks = {turn: along_y(kv, turn) for turn in order[:-1]}
    blocks[0] = kv

    dq = None
    partials = {}
    for turn in order:
        first, last = turn == order[0], turn == order[-1]
        dq_shape = shape(4, ROWS, HD) if last else jax.ShapeDtypeStruct((HD, 4 * ROWS), f32)
        dq, dkv = pl.pallas_call(
            functools.partial(attend, first, last, turn),
            out_shape=(dq_shape, shape(2, 2, TOK, HD)),
            in_specs=[SMEM, SMEM] + [VMEM] * (2 if first else 3),
            out_specs=(VMEM, VMEM),
            compiler_params=PARAMS,
            cost_estimate=FREE,
            name="attend_%d" % turn,
        )(where, block_ids, message, blocks[turn], *(() if first else (dq,)))
        partials[turn] = dkv if turn == 0 else along_y(dkv, -turn)

    dq = lax.all_to_all(dq, ("x_hi", "x_lo"), 0, 0, tiled=True)
    own, other = pl.pallas_call(
        add_partials,
        out_shape=(shape(2, TOK, HD), shape(2, TOK, HD)),
        in_specs=[VMEM] * 4,
        out_specs=(VMEM, VMEM),
        compiler_params=PARAMS,
        name="add_partials",
    )(*(partials[turn] for turn in range(4)))
    own = lax.ppermute(own, names, route(-1, lambda a, c: (a, c)))
    other = lax.ppermute(other, names, route(-1, lambda a, c: (1 - a, c)))
    grad_queries = pl.pallas_call(
        unpack_queries,
        out_shape=shape(TOK, 2 * KVH * HD),
        in_specs=[VMEM],
        out_specs=VMEM,
        compiler_params=PARAMS,
        name="unpack_queries",
    )(dq)
    grad_keys, grad_values = pl.pallas_call(
        unpack_kv,
        out_shape=(shape(TOK, 2 * HD), shape(TOK, 2 * HD)),
        in_specs=[SMEM, VMEM, VMEM],
        out_specs=(HBM, HBM),
        scratch_shapes=[pltpu.SemaphoreType.DMA((4,))],
        compiler_params=PARAMS,
        name="unpack_kv",
    )(where, own, other)
    return grad_queries, grad_keys, grad_values


def solution(mesh):
    inner, outer, head = (mesh.shape[name] for name in ("inner", "outer", "head"))
    fine = Mesh(mesh.devices.reshape(inner // 2, 2, outer, head), ("y", "x_hi", "outer", "x_lo"))
    rows = ("y", "x_hi", "outer")
    in_specs = (
        P(rows, "x_lo"),
        P(rows, None),
        P(rows, None),
        P(rows, "x_lo"),
        P(rows, "x_lo"),
        P("x_lo", rows),
        P(),
    )
    out_specs = (P(rows, "x_lo"), P(rows, "x_lo"), P(rows, "x_lo"))
    return jax.shard_map(per_device, mesh=fine, in_specs=in_specs, out_specs=out_specs, check_vma=False)
```

```python
import functools
import math

import jax
import jax.numpy as jnp
from jax import lax
from jax.experimental import pallas as pl
from jax.experimental.pallas import tpu as pltpu
from jax.sharding import Mesh
from jax.sharding import PartitionSpec as P

KVH = 4
HD = 128
TOK = 256
HALF = 128
SCALE = 1.0 / math.sqrt(HD)
EXP2_SCALE = SCALE * math.log2(math.e)
HIDDEN = 1.0e30
ROWS = 2 * TOK
AUX = 32
NT = (((1,), (1,)), ((), ()))
NN = (((1,), (0,)), ((), ()))
VMEM = pl.BlockSpec(memory_space=pltpu.VMEM)
HBM = pl.BlockSpec(memory_space=pltpu.HBM)
SMEM = pl.BlockSpec(memory_space=pltpu.SMEM)
f32 = jnp.float32
bf16 = jnp.bfloat16
FREE = pl.CostEstimate(flops=0, bytes_accessed=0, transcendentals=0)
LONG = pl.CostEstimate(flops=10**10, bytes_accessed=0, transcendentals=0)
WIDE = pltpu.CompilerParams(vmem_limit_bytes=60 * 2**20)
PARAMS = pltpu.CompilerParams(vmem_limit_bytes=24 * 2**20)


def dot(a, b, dims):
    return lax.dot_general(a, b, dims, preferred_element_type=f32)


def split3(x):
    a = x.astype(bf16)
    r = x - a.astype(f32)
    b = r.astype(bf16)
    c = (r - b.astype(f32)).astype(bf16)
    return a, b, c


def head_of(x):
    return 2 * (x % 2) + x // 2


def pack_queries(queries, attn_out, grad_out, row_total, message, q_in, o_in, g_in, t_in, staged, sems, out_sems):
    copies = [
        pltpu.make_async_copy(source, target, sems.at[i])
        for i, (source, target) in enumerate(((row_total, t_in), (grad_out, g_in), (attn_out, o_in), (queries, q_in)))
    ]
    for copy in copies:
        copy.start()
    ones = jnp.ones((8, HD), bf16)
    copies[0].wait()
    log_total = jnp.log(t_in[...]) * f32(math.log2(math.e))
    copies[1].wait()
    copies[2].wait()
    sends = []
    for x in range(4):
        parts = []
        for n in range(2):
            h = n * KVH + head_of(x)
            columns = slice(h * HD, (h + 1) * HD)
            grad = g_in[:, columns]
            product = grad.astype(f32) * o_in[:, columns].astype(f32)
            high = product.astype(bf16)
            low = (product - high.astype(f32)).astype(bf16)
            delta = (dot(ones, high, NT) + dot(ones, low, NT))[0:1]
            parts.append((log_total[h : h + 1], delta))
            for half in range(2):
                at = ROWS + (half * 2 + n) * HALF
                staged[x, at : at + HALF] = grad[half * HALF : (half + 1) * HALF]
        table = []
        for which in range(2):
            for half in range(2):
                for n in range(2):
                    table.append(parts[n][which][:, half * HALF : (half + 1) * HALF])
        table = jnp.concatenate(table, axis=0)
        a, b, c = split3(table)
        pad = jnp.zeros((8, HALF), bf16)
        staged[x, 2 * ROWS : 2 * ROWS + AUX] = jnp.concatenate([a, b, c, pad], axis=0)
        if x == 0:
            copies[3].wait()
        for n in range(2):
            h = n * KVH + head_of(x)
            for half in range(2):
                at = (half * 2 + n) * HALF
                staged[x, at : at + HALF] = q_in[half * HALF : (half + 1) * HALF, h * HD : (h + 1) * HD]
        sends.append(pltpu.make_async_copy(staged.at[x], message.at[x], out_sems.at[x]))
        sends[-1].start()
    for send in sends:
        send.wait()


def attend(turn, first, last, *refs):
    where, ids, message, kv = refs[:4]
    dq_in = None if first else refs[4]
    dq_out, dkv = refs[-2:]
    y, x_hi, o, outer = where[0], where[1], where[2], where[4]
    key_y = (y - turn) & 3
    key_o = jnp.where(o == 0, outer - 1, o - 1)
    k = kv[:, 0].reshape(2 * TOK, HD)
    v = kv[:, 1].reshape(2 * TOK, HD)
    kt = k.T
    key_blocks = []
    for j in range(2):
        key_x = 1 - x_hi if j == 0 else x_hi
        for half in range(2):
            key_blocks.append(ids[((key_y * 2 + key_x) * outer + key_o) * 2 + half])
    dk = jnp.zeros((2 * TOK, HD), f32)
    dv = jnp.zeros((2 * TOK, HD), f32)
    for x in range(4):
        table = message[x, 2 * ROWS : 2 * ROWS + AUX, :].astype(f32)
        table = table[0:8] + table[8:16] + table[16:24]
        shift = jnp.concatenate([table[i : i + 1] for i in range(4)], axis=1)
        delta = jnp.concatenate([table[i : i + 1] for i in range(4, 8)], axis=1)
        query_blocks = [ids[((y * 2 + x // 2) * outer + o) * 2 + half] for half in range(2)]
        q = message[x, 0:ROWS, :]
        g = message[x, ROWS : 2 * ROWS, :]
        scores = dot(k, q, NT)
        dprob = dot(v, g, NT)
        prob = []
        for i in range(4):
            hide = [
                jnp.full((1, TOK), jnp.where(key_blocks[i] < query_blocks[half], 0.0, HIDDEN).astype(f32))
                for half in range(2)
            ]
            row = shift + jnp.concatenate(hide, axis=1)
            prob.append(jnp.exp2(scores[i * HALF : (i + 1) * HALF] * EXP2_SCALE - row))
        prob = jnp.concatenate(prob, axis=0)
        ds = (prob * (dprob - delta)).astype(bf16)
        dv = dv + dot(prob.astype(bf16), g, NN)
        dk = dk + dot(ds, q, NN)
        at = x * ROWS
        dq = dot(kt, ds, NN)
        if not first:
            dq = dq + dq_in[:, at : at + ROWS]
        if last:
            dq_out[x] = (dq * SCALE).astype(bf16)
        else:
            dq_out[:, at : at + ROWS] = dq
    dkv[:, 0] = (dk * SCALE).astype(dkv.dtype).reshape(2, TOK, HD)
    dkv[:, 1] = dv.astype(dkv.dtype).reshape(2, TOK, HD)


def add_partials(a, b, c, mine, other, own):
    for j, out in ((0, other), (1, own)):
        for i in range(2):
            out[i] = (a[j, i].astype(f32) + b[j, i].astype(f32) + c[j, i].astype(f32) + mine[j, i]).astype(bf16)


def unpack_queries(dq, grad_queries):
    for x in range(4):
        part = dq[x].T
        for n in range(2):
            h = n * KVH + head_of(x)
            for half in range(2):
                at = (half * 2 + n) * HALF
                grad_queries[half * HALF : (half + 1) * HALF, h * HD : (h + 1) * HD] = part[at : at + HALF]


def unpack_kv(where, other, own, grad_keys, grad_values, sems):
    mine = pl.ds(pl.multiple_of(where[1] * HD, HD), HD)
    rest = pl.ds(pl.multiple_of((1 - where[1]) * HD, HD), HD)
    copies = []
    for i, out in ((0, grad_keys), (1, grad_values)):
        for columns, part in ((mine, own), (rest, other)):
            copies.append(pltpu.make_async_copy(part.at[i], out.at[:, columns], sems.at[len(copies)]))
    for copy in copies:
        copy.start()
    for copy in copies:
        copy.wait()


def shape(*dims):
    return jax.ShapeDtypeStruct(dims, bf16)


def per_device(queries, keys, values, attn_out, grad_out, row_total, block_ids):
    y_count = lax.axis_size("y")
    outer = lax.axis_size("outer")
    y = lax.axis_index("y")
    x_hi = lax.axis_index("x_hi")
    o = lax.axis_index("outer")
    x_lo = lax.axis_index("x_lo")
    where = jnp.stack([y, x_hi, o, x_lo, jnp.int32(outer)]).astype(jnp.int32)
    names = ("x_hi", "outer", "x_lo")

    def route(step, turn):
        pairs = []
        for a in range(2):
            for b in range(outer):
                for c in range(2):
                    to_a, to_c = turn(a, c)
                    pairs.append(((a * outer + b) * 2 + c, (to_a * outer + (b + step) % outer) * 2 + to_c))
        return pairs

    def along_y(block, turn):
        return lax.ppermute(block, "y", [(i, (i + turn) % y_count) for i in range(y_count)])

    def columns(head):
        at = head * HD
        return jnp.stack([lax.dynamic_slice(x, (0, at), (TOK, HD)) for x in (keys, values)])

    other = columns(2 * (1 - x_lo) + (1 - x_hi))
    own = columns(2 * x_lo + x_hi)
    other = lax.ppermute(other, names, route(1, lambda a, c: (1 - a, 1 - c)))
    own = lax.ppermute(own, names, route(1, lambda a, c: (a, c)))

    message = pl.pallas_call(
        pack_queries,
        out_shape=shape(4, 2 * ROWS + AUX, HD),
        in_specs=[HBM] * 4,
        out_specs=HBM,
        scratch_shapes=[pltpu.VMEM((TOK, 2 * KVH * HD), bf16)] * 3
        + [
            pltpu.VMEM((2 * KVH, TOK), f32),
            pltpu.VMEM((4, 2 * ROWS + AUX, HD), bf16),
            pltpu.SemaphoreType.DMA((4,)),
            pltpu.SemaphoreType.DMA((4,)),
        ],
        compiler_params=WIDE,
        name="pack_queries",
    )(queries, attn_out, grad_out, row_total)
    other, own, message = lax.optimization_barrier((other, own, message))
    message = lax.all_to_all(message, ("x_hi", "x_lo"), 0, 0, tiled=True)

    kv = jnp.stack([other, own])
    turns = (1, 3, 2)
    blocks = [along_y(kv, turn) for turn in turns] + [kv]
    dq = None
    parts = []
    for turn, block in zip(turns + (0,), blocks):
        first, last = turn == turns[0], turn == 0
        dq, dkv = pl.pallas_call(
            functools.partial(attend, turn, first, last),
            out_shape=(
                shape(4, HD, ROWS) if last else jax.ShapeDtypeStruct((HD, 4 * ROWS), f32),
                jax.ShapeDtypeStruct((2, 2, TOK, HD), f32 if last else bf16),
            ),
            in_specs=[SMEM, SMEM] + [VMEM] * (2 if first else 3),
            out_specs=(VMEM, VMEM),
            compiler_params=PARAMS,
            cost_estimate=FREE,
            name="attend_%d" % turn,
        )(where, block_ids, message, block, *(() if first else (dq,)))
        parts.append(dkv if last else along_y(dkv, -turn))
    dq = lax.all_to_all(dq, ("x_hi", "x_lo"), 0, 0, tiled=True)
    other, own = pl.pallas_call(
        add_partials,
        out_shape=(shape(2, TOK, HD), shape(2, TOK, HD)),
        in_specs=[VMEM] * 4,
        out_specs=(VMEM, VMEM),
        compiler_params=PARAMS,
        name="add_partials",
    )(*parts)
    other = lax.ppermute(other, names, route(-1, lambda a, c: (1 - a, c)))
    own = lax.ppermute(own, names, route(-1, lambda a, c: (a, c)))
    grad_queries = pl.pallas_call(
        unpack_queries,
        out_shape=shape(TOK, 2 * KVH * HD),
        in_specs=[VMEM],
        out_specs=VMEM,
        compiler_params=PARAMS,
        name="unpack_queries",
    )(dq)
    grad_keys, grad_values = pl.pallas_call(
        unpack_kv,
        out_shape=(shape(TOK, 2 * HD), shape(TOK, 2 * HD)),
        in_specs=[SMEM, VMEM, VMEM],
        out_specs=(HBM, HBM),
        scratch_shapes=[pltpu.SemaphoreType.DMA((4,))],
        compiler_params=PARAMS,
        name="unpack_kv",
    )(where, other, own)
    return grad_queries, grad_keys, grad_values


def solution(mesh):
    inner, outer, head = (mesh.shape[name] for name in ("inner", "outer", "head"))
    fine = Mesh(mesh.devices.reshape(inner // 2, 2, outer, head), ("y", "x_hi", "outer", "x_lo"))
    rows = ("y", "x_hi", "outer")
    in_specs = (
        P(rows, "x_lo"),
        P(rows, None),
        P(rows, None),
        P(rows, "x_lo"),
        P(rows, "x_lo"),
        P("x_lo", rows),
        P(),
    )
    out_specs = (P(rows, "x_lo"), P(rows, "x_lo"), P(rows, "x_lo"))
    return jax.shard_map(per_device, mesh=fine, in_specs=in_specs, out_specs=out_specs, check_vma=False)
```

```python
import functools
import math

import jax
import jax.numpy as jnp
from jax import lax
from jax.experimental import pallas as pl
from jax.experimental.pallas import tpu as pltpu
from jax.sharding import Mesh
from jax.sharding import PartitionSpec as P

KVH = 4
HD = 128
TOK = 256
HALF = 128
SCALE = 1.0 / math.sqrt(HD)
EXP2_SCALE = SCALE * math.log2(math.e)
HIDDEN = 1.0e30
ROWS = 2 * TOK
AUX = 32
NT = (((1,), (1,)), ((), ()))
NN = (((1,), (0,)), ((), ()))
VMEM = pl.BlockSpec(memory_space=pltpu.VMEM)
HBM = pl.BlockSpec(memory_space=pltpu.HBM)
SMEM = pl.BlockSpec(memory_space=pltpu.SMEM)
f32 = jnp.float32
bf16 = jnp.bfloat16
LONG = pl.CostEstimate(flops=2 * 10**10, bytes_accessed=0, transcendentals=0)
LONG = pl.CostEstimate(flops=10**10, bytes_accessed=0, transcendentals=0)
WIDE = pltpu.CompilerParams(vmem_limit_bytes=60 * 2**20)
PARAMS = pltpu.CompilerParams(vmem_limit_bytes=24 * 2**20)


def dot(a, b, dims):
    return lax.dot_general(a, b, dims, preferred_element_type=f32)


def split3(x):
    a = x.astype(bf16)
    r = x - a.astype(f32)
    b = r.astype(bf16)
    c = (r - b.astype(f32)).astype(bf16)
    return a, b, c


def head_of(x):
    return 2 * (x % 2) + x // 2


def pack_queries(queries, attn_out, grad_out, row_total, message, q_in, o_in, g_in, t_in, staged, sems, out_sems):
    copies = [
        pltpu.make_async_copy(source, target, sems.at[i])
        for i, (source, target) in enumerate(((row_total, t_in), (grad_out, g_in), (attn_out, o_in), (queries, q_in)))
    ]
    for copy in copies:
        copy.start()
    ones = jnp.ones((8, HD), bf16)
    copies[0].wait()
    log_total = jnp.log(t_in[...]) * f32(math.log2(math.e))
    copies[1].wait()
    copies[2].wait()
    sends = []
    for x in range(4):
        parts = []
        for n in range(2):
            h = n * KVH + head_of(x)
            columns = slice(h * HD, (h + 1) * HD)
            grad = g_in[:, columns]
            product = grad.astype(f32) * o_in[:, columns].astype(f32)
            high = product.astype(bf16)
            low = (product - high.astype(f32)).astype(bf16)
            delta = (dot(ones, high, NT) + dot(ones, low, NT))[0:1]
            parts.append((log_total[h : h + 1], delta))
            for half in range(2):
                at = ROWS + (half * 2 + n) * HALF
                staged[x, at : at + HALF] = grad[half * HALF : (half + 1) * HALF]
        table = []
        for which in range(2):
            for half in range(2):
                for n in range(2):
                    table.append(parts[n][which][:, half * HALF : (half + 1) * HALF])
        table = jnp.concatenate(table, axis=0)
        a, b, c = split3(table)
        pad = jnp.zeros((8, HALF), bf16)
        staged[x, 2 * ROWS : 2 * ROWS + AUX] = jnp.concatenate([a, b, c, pad], axis=0)
        if x == 0:
            copies[3].wait()
        for n in range(2):
            h = n * KVH + head_of(x)
            for half in range(2):
                at = (half * 2 + n) * HALF
                staged[x, at : at + HALF] = q_in[half * HALF : (half + 1) * HALF, h * HD : (h + 1) * HD]
        sends.append(pltpu.make_async_copy(staged.at[x], message.at[x], out_sems.at[x]))
        sends[-1].start()
    for send in sends:
        send.wait()


def attend(turn, first, last, *refs):
    hide, message, kv = refs[:3]
    dq_in = None if first else refs[3]
    dq_out, dkv, rows = refs[-3:]
    k = kv[:, 0].reshape(2 * TOK, HD)
    v = kv[:, 1].reshape(2 * TOK, HD)
    kt = k.T
    for x in range(4):
        table = message[x, 2 * ROWS : 2 * ROWS + AUX, :].astype(f32)
        table = table[0:8] + table[8:16] + table[16:24]
        for c in range(4):
            lanes = slice(c * HALF, (c + 1) * HALF)
            for i in range(4):
                rows[i, x : x + 1, lanes] = table[c : c + 1] + hide[turn, i, x : x + 1, lanes]
            rows[4, x : x + 1, lanes] = table[4 + c : 5 + c]
    dk = dv = None
    for x in range(4):
        q = message[x, 0:ROWS, :]
        g = message[x, ROWS : 2 * ROWS, :]
        scores = dot(k, q, NT)
        dprob = dot(v, g, NT)
        prob = jnp.concatenate(
            [
                jnp.exp2(scores[i * HALF : (i + 1) * HALF] * EXP2_SCALE - rows[i, x : x + 1, :])
                for i in range(4)
            ],
            axis=0,
        )
        ds = (prob * (dprob - rows[4, x : x + 1, :])).astype(bf16)
        dv_part = dot(prob.astype(bf16), g, NN)
        dk_part = dot(ds, q, NN)
        dv = dv_part if dv is None else dv + dv_part
        dk = dk_part if dk is None else dk + dk_part
        at = x * ROWS
        dq = dot(kt, ds, NN)
        if not first:
            dq = dq + dq_in[:, at : at + ROWS]
        if last:
            dq_out[x] = (dq * SCALE).astype(bf16)
        else:
            dq_out[:, at : at + ROWS] = dq
    dkv[:, 0] = (dk * SCALE).astype(dkv.dtype).reshape(2, TOK, HD)
    dkv[:, 1] = dv.astype(dkv.dtype).reshape(2, TOK, HD)


def add_partials(mine, a, b, c, other, own):
    for j, out in ((0, own), (1, other)):
        for i in range(2):
            out[i] = (a[j, i].astype(f32) + b[j, i].astype(f32) + c[j, i].astype(f32) + mine[j, i]).astype(bf16)


def unpack_queries(dq, grad_queries):
    for x in range(4):
        part = dq[x].T
        for n in range(2):
            h = n * KVH + head_of(x)
            for half in range(2):
                at = (half * 2 + n) * HALF
                grad_queries[half * HALF : (half + 1) * HALF, h * HD : (h + 1) * HD] = part[at : at + HALF]


def unpack_kv(swap, other, own, grad_keys, grad_values):
    second = swap[0:1, :] > 0
    for i, out in ((0, grad_keys), (1, grad_values)):
        out[:, 0:HD] = jnp.where(second, other[i], own[i])
        out[:, HD : 2 * HD] = jnp.where(second, own[i], other[i])


def shape(*dims):
    return jax.ShapeDtypeStruct(dims, bf16)


def per_device(queries, keys, values, attn_out, grad_out, row_total, block_ids):
    y_count = lax.axis_size("y")
    outer = lax.axis_size("outer")
    y = lax.axis_index("y")
    x_hi = lax.axis_index("x_hi")
    o = lax.axis_index("outer")
    x_lo = lax.axis_index("x_lo")
    names = ("x_hi", "outer", "x_lo")

    def route(step, turn):
        pairs = []
        for a in range(2):
            for b in range(outer):
                for c in range(2):
                    to_a, to_c = turn(a, c)
                    pairs.append(((a * outer + b) * 2 + c, (to_a * outer + (b + step) % outer) * 2 + to_c))
        return pairs

    def along_y(block, turn):
        return lax.ppermute(block, "y", [(i, (i + turn) % y_count) for i in range(y_count)])

    def columns(head):
        at = head * HD
        return jnp.stack([lax.dynamic_slice(x, (0, at), (TOK, HD)) for x in (keys, values)])

    other = columns(2 * (1 - x_lo) + (1 - x_hi))
    own = columns(2 * x_lo + x_hi)
    other, row_total = lax.optimization_barrier((other, row_total))
    other = lax.ppermute(other, names, route(1, lambda a, c: (1 - a, 1 - c)))

    message = pl.pallas_call(
        pack_queries,
        out_shape=shape(4, 2 * ROWS + AUX, HD),
        in_specs=[HBM] * 4,
        out_specs=HBM,
        scratch_shapes=[pltpu.VMEM((TOK, 2 * KVH * HD), bf16)] * 3
        + [
            pltpu.VMEM((2 * KVH, TOK), f32),
            pltpu.VMEM((4, 2 * ROWS + AUX, HD), bf16),
            pltpu.SemaphoreType.DMA((4,)),
            pltpu.SemaphoreType.DMA((4,)),
        ],
        compiler_params=WIDE,
        name="pack_queries",
    )(queries, attn_out, grad_out, row_total)
    own, other = lax.optimization_barrier((own, other))
    own = lax.ppermute(own, names, route(1, lambda a, c: (a, c)))
    message = lax.all_to_all(message, ("x_hi", "x_lo"), 0, 0, tiled=True)

    kv = jnp.stack([own, other])
    stored = block_ids.reshape(y_count, 2, outer, 2)
    query_ids = lax.dynamic_slice(stored, (y, 0, o, 0), (1, 2, 1, 2)).reshape(2, 2)
    key_ids = lax.dynamic_slice(stored, (0, 0, (o + outer - 1) % outer, 0), (y_count, 2, 1, 2)).reshape(y_count, 2, 2)
    key_ids = jnp.concatenate([key_ids[::-1]] * 2)
    key_ids = lax.dynamic_slice(key_ids, (y_count - 1 - y, 0, 0), (y_count, 2, 2))
    key_ids = jnp.where(x_hi == 0, key_ids, key_ids[:, ::-1]).reshape(y_count, 4, 1, 1)
    visible = key_ids < jnp.repeat(query_ids, 2, axis=0).reshape(1, 1, 4, 2)
    hide = jnp.repeat(jnp.where(visible, f32(0.0), f32(HIDDEN)), TOK, axis=3)

    turns = (1, 3, 2)
    blocks = [kv] + [along_y(kv, turn) for turn in turns]
    dq = None
    parts = []
    for turn, block in zip((0,) + turns, blocks):
        first, last = turn == 0, turn == turns[-1]
        dq, dkv = pl.pallas_call(
            functools.partial(attend, turn, first, last),
            out_shape=(
                shape(4, HD, ROWS) if last else jax.ShapeDtypeStruct((HD, 4 * ROWS), f32),
                jax.ShapeDtypeStruct((2, 2, TOK, HD), f32 if first else bf16),
            ),
            in_specs=[VMEM] * (3 if first else 4),
            out_specs=(VMEM, VMEM),
            compiler_params=PARAMS,
            scratch_shapes=[pltpu.VMEM((5, 4, ROWS), f32)],
            cost_estimate=LONG,
            name="attend_%d" % turn,
        )(hide, message, block, *(() if first else (dq,)))
        parts.append(dkv if first else along_y(dkv, -turn))
    dq = lax.all_to_all(dq, ("x_hi", "x_lo"), 0, 0, tiled=True)
    other, own = pl.pallas_call(
        add_partials,
        out_shape=(shape(2, TOK, HD), shape(2, TOK, HD)),
        in_specs=[VMEM] * 4,
        out_specs=(VMEM, VMEM),
        compiler_params=PARAMS,
        name="add_partials",
    )(*parts)
    other = lax.ppermute(other, names, route(-1, lambda a, c: (1 - a, c)))
    own = lax.ppermute(own, names, route(-1, lambda a, c: (a, c)))
    grad_queries = pl.pallas_call(
        unpack_queries,
        out_shape=shape(TOK, 2 * KVH * HD),
        in_specs=[VMEM],
        out_specs=VMEM,
        compiler_params=PARAMS,
        name="unpack_queries",
    )(dq)
    grad_keys, grad_values = pl.pallas_call(
        unpack_kv,
        out_shape=(shape(TOK, 2 * HD), shape(TOK, 2 * HD)),
        in_specs=[VMEM] * 3,
        out_specs=(VMEM, VMEM),
        compiler_params=PARAMS,
        name="unpack_kv",
    )(jnp.full((8, HD), x_hi, jnp.int32), other, own)
    return grad_queries, grad_keys, grad_values


def solution(mesh):
    inner, outer, head = (mesh.shape[name] for name in ("inner", "outer", "head"))
    fine = Mesh(mesh.devices.reshape(inner // 2, 2, outer, head), ("y", "x_hi", "outer", "x_lo"))
    rows = ("y", "x_hi", "outer")
    in_specs = (
        P(rows, "x_lo"),
        P(rows, None),
        P(rows, None),
        P(rows, "x_lo"),
        P(rows, "x_lo"),
        P("x_lo", rows),
        P(),
    )
    out_specs = (P(rows, "x_lo"), P(rows, "x_lo"), P(rows, "x_lo"))
    return jax.shard_map(per_device, mesh=fine, in_specs=in_specs, out_specs=out_specs, check_vma=False)
```

```python
import functools
import math

import jax
import jax.numpy as jnp
from jax import lax
from jax.experimental import pallas as pl
from jax.experimental.pallas import tpu as pltpu
from jax.sharding import Mesh
from jax.sharding import PartitionSpec as P

KVH = 4
HD = 128
TOK = 256
HALF = 128
SCALE = 1.0 / math.sqrt(HD)
EXP2_SCALE = SCALE * math.log2(math.e)
HIDDEN = 1.0e30
ROWS = 2 * TOK
AUX = 32
NT = (((1,), (1,)), ((), ()))
NN = (((1,), (0,)), ((), ()))
VMEM = pl.BlockSpec(memory_space=pltpu.VMEM)
HBM = pl.BlockSpec(memory_space=pltpu.HBM)
SMEM = pl.BlockSpec(memory_space=pltpu.SMEM)
f32 = jnp.float32
bf16 = jnp.bfloat16
LONG = pl.CostEstimate(flops=2 * 10**10, bytes_accessed=0, transcendentals=0)
LONG = pl.CostEstimate(flops=10**10, bytes_accessed=0, transcendentals=0)
WIDE = pltpu.CompilerParams(vmem_limit_bytes=60 * 2**20)
PARAMS = pltpu.CompilerParams(vmem_limit_bytes=24 * 2**20)


def dot(a, b, dims):
    return lax.dot_general(a, b, dims, preferred_element_type=f32)


def split3(x):
    a = x.astype(bf16)
    r = x - a.astype(f32)
    b = r.astype(bf16)
    c = (r - b.astype(f32)).astype(bf16)
    return a, b, c


def head_of(x):
    return 2 * (x % 2) + x // 2


def pack_queries(queries, attn_out, grad_out, row_total, message, q_in, o_in, g_in, t_in, staged, sems, out_sems):
    copies = [
        pltpu.make_async_copy(source, target, sems.at[i])
        for i, (source, target) in enumerate(((row_total, t_in), (grad_out, g_in), (attn_out, o_in), (queries, q_in)))
    ]
    for copy in copies:
        copy.start()
    ones = jnp.ones((8, HD), bf16)
    copies[0].wait()
    log_total = jnp.log(t_in[...]) * f32(math.log2(math.e))
    copies[1].wait()
    copies[2].wait()
    sends = []
    for x in range(4):
        parts = []
        for n in range(2):
            h = n * KVH + head_of(x)
            columns = slice(h * HD, (h + 1) * HD)
            grad = g_in[:, columns]
            product = grad.astype(f32) * o_in[:, columns].astype(f32)
            high = product.astype(bf16)
            low = (product - high.astype(f32)).astype(bf16)
            delta = (dot(ones, high, NT) + dot(ones, low, NT))[0:1]
            parts.append((log_total[h : h + 1], delta))
            for half in range(2):
                at = ROWS + (half * 2 + n) * HALF
                staged[x, at : at + HALF] = grad[half * HALF : (half + 1) * HALF]
        table = []
        for which in range(2):
            for half in range(2):
                for n in range(2):
                    table.append(parts[n][which][:, half * HALF : (half + 1) * HALF])
        table = jnp.concatenate(table, axis=0)
        a, b, c = split3(table)
        pad = jnp.zeros((8, HALF), bf16)
        staged[x, 2 * ROWS : 2 * ROWS + AUX] = jnp.concatenate([a, b, c, pad], axis=0)
        if x == 0:
            copies[3].wait()
        for n in range(2):
            h = n * KVH + head_of(x)
            for half in range(2):
                at = (half * 2 + n) * HALF
                staged[x, at : at + HALF] = q_in[half * HALF : (half + 1) * HALF, h * HD : (h + 1) * HD]
        sends.append(pltpu.make_async_copy(staged.at[x], message.at[x], out_sems.at[x]))
        sends[-1].start()
    for send in sends:
        send.wait()


def attend(turn, first, last, *refs):
    hide, message, kv = refs[:3]
    dq_in = None if first else refs[3]
    dq_out, dkv, rows = refs[-3:]
    k = kv[:, 0].reshape(2 * TOK, HD)
    v = kv[:, 1].reshape(2 * TOK, HD)
    kt = k.T
    for x in range(4):
        table = message[x, 2 * ROWS : 2 * ROWS + AUX, :].astype(f32)
        table = table[0:8] + table[8:16] + table[16:24]
        for c in range(4):
            lanes = slice(c * HALF, (c + 1) * HALF)
            for i in range(4):
                rows[i, x : x + 1, lanes] = table[c : c + 1] + hide[turn, i, x : x + 1, lanes]
            rows[4, x : x + 1, lanes] = table[4 + c : 5 + c]
    dk = dv = None
    for x in range(4):
        q = message[x, 0:ROWS, :]
        g = message[x, ROWS : 2 * ROWS, :]
        scores = dot(k, q, NT)
        dprob = dot(v, g, NT)
        prob = jnp.concatenate(
            [
                jnp.exp2(scores[i * HALF : (i + 1) * HALF] * EXP2_SCALE - rows[i, x : x + 1, :])
                for i in range(4)
            ],
            axis=0,
        )
        ds = (prob * (dprob - rows[4, x : x + 1, :])).astype(bf16)
        dv_part = dot(prob.astype(bf16), g, NN)
        dk_part = dot(ds, q, NN)
        dv = dv_part if dv is None else dv + dv_part
        dk = dk_part if dk is None else dk + dk_part
        at = x * ROWS
        dq = dot(kt, ds, NN)
        if not first:
            dq = dq + dq_in[:, at : at + ROWS]
        if last:
            dq_out[x] = (dq * SCALE).astype(bf16)
        else:
            dq_out[:, at : at + ROWS] = dq
    dkv[:, 0] = (dk * SCALE).astype(dkv.dtype).reshape(2, TOK, HD)
    dkv[:, 1] = dv.astype(dkv.dtype).reshape(2, TOK, HD)


def add_partials(mine, a, b, c, other, own):
    for j, out in ((0, own), (1, other)):
        for i in range(2):
            out[i] = (a[j, i].astype(f32) + b[j, i].astype(f32) + c[j, i].astype(f32) + mine[j, i]).astype(bf16)


def unpack_queries(dq, grad_queries):
    for x in range(4):
        part = dq[x].T
        for n in range(2):
            h = n * KVH + head_of(x)
            for half in range(2):
                at = (half * 2 + n) * HALF
                grad_queries[half * HALF : (half + 1) * HALF, h * HD : (h + 1) * HD] = part[at : at + HALF]


def unpack_kv(swap, other, own, grad_keys, grad_values):
    second = swap[0:1, :] > 0
    for i, out in ((0, grad_keys), (1, grad_values)):
        out[:, 0:HD] = jnp.where(second, other[i], own[i])
        out[:, HD : 2 * HD] = jnp.where(second, own[i], other[i])


def shape(*dims):
    return jax.ShapeDtypeStruct(dims, bf16)


def per_device(queries, keys, values, attn_out, grad_out, row_total, block_ids):
    y_count = lax.axis_size("y")
    outer = lax.axis_size("outer")
    y = lax.axis_index("y")
    x_hi = lax.axis_index("x_hi")
    o = lax.axis_index("outer")
    x_lo = lax.axis_index("x_lo")
    names = ("x_hi", "outer", "x_lo")

    def route(step, turn):
        pairs = []
        for a in range(2):
            for b in range(outer):
                for c in range(2):
                    to_a, to_c = turn(a, c)
                    pairs.append(((a * outer + b) * 2 + c, (to_a * outer + (b + step) % outer) * 2 + to_c))
        return pairs

    def along_y(block, turn):
        return lax.ppermute(block, "y", [(i, (i + turn) % y_count) for i in range(y_count)])

    def columns(head):
        at = head * HD
        return jnp.stack([lax.dynamic_slice(x, (0, at), (TOK, HD)) for x in (keys, values)])

    other = columns(2 * (1 - x_lo) + (1 - x_hi))
    own = columns(2 * x_lo + x_hi)
    other, row_total = lax.optimization_barrier((other, row_total))
    other = lax.ppermute(other, names, route(1, lambda a, c: (1 - a, 1 - c)))

    message = pl.pallas_call(
        pack_queries,
        out_shape=shape(4, 2 * ROWS + AUX, HD),
        in_specs=[HBM] * 4,
        out_specs=HBM,
        scratch_shapes=[pltpu.VMEM((TOK, 2 * KVH * HD), bf16)] * 3
        + [
            pltpu.VMEM((2 * KVH, TOK), f32),
            pltpu.VMEM((4, 2 * ROWS + AUX, HD), bf16),
            pltpu.SemaphoreType.DMA((4,)),
            pltpu.SemaphoreType.DMA((4,)),
        ],
        compiler_params=WIDE,
        name="pack_queries",
    )(queries, attn_out, grad_out, row_total)
    own, message = lax.optimization_barrier((own, message))
    own = lax.ppermute(own, names, route(1, lambda a, c: (a, c)))
    other, message = lax.optimization_barrier((other, message))
    message = lax.all_to_all(message, ("x_hi", "x_lo"), 0, 0, tiled=True)

    kv = jnp.stack([own, other])
    stored = block_ids.reshape(y_count, 2, outer, 2)
    query_ids = lax.dynamic_slice(stored, (y, 0, o, 0), (1, 2, 1, 2)).reshape(2, 2)
    key_ids = lax.dynamic_slice(stored, (0, 0, (o + outer - 1) % outer, 0), (y_count, 2, 1, 2)).reshape(y_count, 2, 2)
    key_ids = jnp.concatenate([key_ids[::-1]] * 2)
    key_ids = lax.dynamic_slice(key_ids, (y_count - 1 - y, 0, 0), (y_count, 2, 2))
    key_ids = jnp.where(x_hi == 0, key_ids, key_ids[:, ::-1]).reshape(y_count, 4, 1, 1)
    visible = key_ids < jnp.repeat(query_ids, 2, axis=0).reshape(1, 1, 4, 2)
    hide = jnp.repeat(jnp.where(visible, f32(0.0), f32(HIDDEN)), TOK, axis=3)

    turns = (1, 2, 3)
    blocks = [along_y(kv, turn) for turn in turns] + [kv]
    dq = None
    parts = []
    for turn, block in zip(turns + (0,), blocks):
        first, last = turn == turns[0], turn == 0
        dq, dkv = pl.pallas_call(
            functools.partial(attend, turn, first, last),
            out_shape=(
                shape(4, HD, ROWS) if last else jax.ShapeDtypeStruct((HD, 4 * ROWS), f32),
                jax.ShapeDtypeStruct((2, 2, TOK, HD), f32 if last else bf16),
            ),
            in_specs=[VMEM] * (3 if first else 4),
            out_specs=(VMEM, VMEM),
            compiler_params=PARAMS,
            scratch_shapes=[pltpu.VMEM((5, 4, ROWS), f32)],
            cost_estimate=LONG,
            name="attend_%d" % turn,
        )(hide, message, block, *(() if first else (dq,)))
        parts.append(dkv)
    def along_cores(block, step):
        axes = ("y", "outer")
        pairs = []
        for a in range(y_count):
            for b in range(outer):
                to_a, to_b = (a, b + 1) if b % 2 == 0 else ((a + 1) % y_count, b - 1)
                pair = (a * outer + b, to_a * outer + to_b)
                pairs.append(pair if step == 1 else pair[::-1])
        return lax.ppermute(block, axes, pairs)

    before, opposite, after, mine = parts
    before = along_cores(before, -1)
    after = along_cores(after, 1)
    opposite = along_y(opposite, 2)
    before, after, dq = lax.optimization_barrier((before, after, dq))
    before = along_cores(before, -1)
    after = along_cores(after, 1)
    dq = lax.all_to_all(dq, ("x_hi", "x_lo"), 0, 0, tiled=True)
    other, own = pl.pallas_call(
        add_partials,
        out_shape=(shape(2, TOK, HD), shape(2, TOK, HD)),
        in_specs=[VMEM] * 4,
        out_specs=(VMEM, VMEM),
        compiler_params=PARAMS,
        name="add_partials",
    )(mine, before, after, opposite)
    other = lax.ppermute(other, names, route(-1, lambda a, c: (1 - a, c)))
    own = lax.ppermute(own, names, route(-1, lambda a, c: (a, c)))
    grad_queries = pl.pallas_call(
        unpack_queries,
        out_shape=shape(TOK, 2 * KVH * HD),
        in_specs=[VMEM],
        out_specs=VMEM,
        compiler_params=PARAMS,
        name="unpack_queries",
    )(dq)
    grad_keys, grad_values = pl.pallas_call(
        unpack_kv,
        out_shape=(shape(TOK, 2 * HD), shape(TOK, 2 * HD)),
        in_specs=[VMEM] * 3,
        out_specs=(VMEM, VMEM),
        compiler_params=PARAMS,
        name="unpack_kv",
    )(jnp.full((8, HD), x_hi, jnp.int32), other, own)
    return grad_queries, grad_keys, grad_values


def solution(mesh):
    inner, outer, head = (mesh.shape[name] for name in ("inner", "outer", "head"))
    fine = Mesh(mesh.devices.reshape(inner // 2, 2, outer, head), ("y", "x_hi", "outer", "x_lo"))
    rows = ("y", "x_hi", "outer")
    in_specs = (
        P(rows, "x_lo"),
        P(rows, None),
        P(rows, None),
        P(rows, "x_lo"),
        P(rows, "x_lo"),
        P("x_lo", rows),
        P(),
    )
    out_specs = (P(rows, "x_lo"), P(rows, "x_lo"), P(rows, "x_lo"))
    return jax.shard_map(per_device, mesh=fine, in_specs=in_specs, out_specs=out_specs, check_vma=False)
```

```python
import functools
import math

import jax
import jax.numpy as jnp
from jax import lax
from jax.experimental import pallas as pl
from jax.experimental.pallas import tpu as pltpu
from jax.sharding import Mesh
from jax.sharding import PartitionSpec as P

KVH = 4
HD = 128
TOK = 256
HALF = 128
SCALE = 1.0 / math.sqrt(HD)
EXP2_SCALE = SCALE * math.log2(math.e)
HIDDEN = 1.0e30
ROWS = 2 * TOK
AUX = 32
NT = (((1,), (1,)), ((), ()))
NN = (((1,), (0,)), ((), ()))
VMEM = pl.BlockSpec(memory_space=pltpu.VMEM)
HBM = pl.BlockSpec(memory_space=pltpu.HBM)
SMEM = pl.BlockSpec(memory_space=pltpu.SMEM)
f32 = jnp.float32
bf16 = jnp.bfloat16
LONG = pl.CostEstimate(flops=2 * 10**10, bytes_accessed=0, transcendentals=0)
LONG = pl.CostEstimate(flops=10**10, bytes_accessed=0, transcendentals=0)
WIDE = pltpu.CompilerParams(vmem_limit_bytes=60 * 2**20)
PARAMS = pltpu.CompilerParams(vmem_limit_bytes=24 * 2**20)


def dot(a, b, dims):
    return lax.dot_general(a, b, dims, preferred_element_type=f32)


def split3(x):
    a = x.astype(bf16)
    r = x - a.astype(f32)
    b = r.astype(bf16)
    c = (r - b.astype(f32)).astype(bf16)
    return a, b, c


def head_of(x):
    return 2 * (x % 2) + x // 2


def pack_queries(queries, attn_out, grad_out, row_total, message, q_in, o_in, g_in, t_in, staged, sems, out_sems):
    copies = [
        pltpu.make_async_copy(source, target, sems.at[i])
        for i, (source, target) in enumerate(((row_total, t_in), (grad_out, g_in), (attn_out, o_in), (queries, q_in)))
    ]
    for copy in copies:
        copy.start()
    ones = jnp.ones((8, HD), bf16)
    copies[0].wait()
    log_total = jnp.log(t_in[...]) * f32(math.log2(math.e))
    copies[1].wait()
    copies[2].wait()
    sends = []
    for x in range(4):
        parts = []
        for n in range(2):
            h = n * KVH + head_of(x)
            columns = slice(h * HD, (h + 1) * HD)
            grad = g_in[:, columns]
            product = grad.astype(f32) * o_in[:, columns].astype(f32)
            high = product.astype(bf16)
            low = (product - high.astype(f32)).astype(bf16)
            delta = (dot(ones, high, NT) + dot(ones, low, NT))[0:1]
            parts.append((log_total[h : h + 1], delta))
            for half in range(2):
                at = ROWS + (half * 2 + n) * HALF
                staged[x, at : at + HALF] = grad[half * HALF : (half + 1) * HALF]
        table = []
        for which in range(2):
            for half in range(2):
                for n in range(2):
                    table.append(parts[n][which][:, half * HALF : (half + 1) * HALF])
        table = jnp.concatenate(table, axis=0)
        a, b, c = split3(table)
        pad = jnp.zeros((8, HALF), bf16)
        staged[x, 2 * ROWS : 2 * ROWS + AUX] = jnp.concatenate([a, b, c, pad], axis=0)
        if x == 0:
            copies[3].wait()
        for n in range(2):
            h = n * KVH + head_of(x)
            for half in range(2):
                at = (half * 2 + n) * HALF
                staged[x, at : at + HALF] = q_in[half * HALF : (half + 1) * HALF, h * HD : (h + 1) * HD]
        sends.append(pltpu.make_async_copy(staged.at[x], message.at[x], out_sems.at[x]))
        sends[-1].start()
    for send in sends:
        send.wait()


def attend(turn, first, last, *refs):
    hide, message, kv = refs[:3]
    dq_in = None if first else refs[3]
    dq_out, dkv, rows = refs[-3:]
    k = kv[:, 0].reshape(2 * TOK, HD)
    v = kv[:, 1].reshape(2 * TOK, HD)
    kt = k.T
    for x in range(4):
        table = message[x, 2 * ROWS : 2 * ROWS + AUX, :].astype(f32)
        table = table[0:8] + table[8:16] + table[16:24]
        for c in range(4):
            lanes = slice(c * HALF, (c + 1) * HALF)
            for i in range(4):
                rows[i, x : x + 1, lanes] = table[c : c + 1] + hide[turn, i, x : x + 1, lanes]
            rows[4, x : x + 1, lanes] = table[4 + c : 5 + c]
    dk = dv = None
    for x in range(4):
        q = message[x, 0:ROWS, :]
        g = message[x, ROWS : 2 * ROWS, :]
        scores = dot(k, q, NT)
        dprob = dot(v, g, NT)
        prob = jnp.concatenate(
            [
                jnp.exp2(scores[i * HALF : (i + 1) * HALF] * EXP2_SCALE - rows[i, x : x + 1, :])
                for i in range(4)
            ],
            axis=0,
        )
        ds = (prob * (dprob - rows[4, x : x + 1, :])).astype(bf16)
        dv_part = dot(prob.astype(bf16), g, NN)
        dk_part = dot(ds, q, NN)
        dv = dv_part if dv is None else dv + dv_part
        dk = dk_part if dk is None else dk + dk_part
        at = x * ROWS
        dq = dot(kt, ds, NN)
        if not first:
            dq = dq + dq_in[:, at : at + ROWS]
        if last:
            dq_out[x] = (dq * SCALE).astype(bf16)
        else:
            dq_out[:, at : at + ROWS] = dq
    dkv[:, 0] = (dk * SCALE).astype(dkv.dtype).reshape(2, TOK, HD)
    dkv[:, 1] = dv.astype(dkv.dtype).reshape(2, TOK, HD)


def add_partials(mine, a, b, c, other, own):
    for j, out in ((0, other), (1, own)):
        for i in range(2):
            out[i] = (a[j, i].astype(f32) + b[j, i].astype(f32) + c[j, i].astype(f32) + mine[j, i]).astype(bf16)


def unpack_queries(dq, grad_queries):
    for x in range(4):
        part = dq[x].T
        for n in range(2):
            h = n * KVH + head_of(x)
            for half in range(2):
                at = (half * 2 + n) * HALF
                grad_queries[half * HALF : (half + 1) * HALF, h * HD : (h + 1) * HD] = part[at : at + HALF]


def unpack_kv(swap, other, own, grad_keys, grad_values):
    second = swap[0:1, :] > 0
    for i, out in ((0, grad_keys), (1, grad_values)):
        out[:, 0:HD] = jnp.where(second, other[i], own[i])
        out[:, HD : 2 * HD] = jnp.where(second, own[i], other[i])


def shape(*dims):
    return jax.ShapeDtypeStruct(dims, bf16)


def per_device(queries, keys, values, attn_out, grad_out, row_total, block_ids):
    y_count = lax.axis_size("y")
    outer = lax.axis_size("outer")
    y = lax.axis_index("y")
    x_hi = lax.axis_index("x_hi")
    o = lax.axis_index("outer")
    x_lo = lax.axis_index("x_lo")
    names = ("x_hi", "outer", "x_lo")

    def route(step, turn):
        pairs = []
        for a in range(2):
            for b in range(outer):
                for c in range(2):
                    to_a, to_c = turn(a, c)
                    pairs.append(((a * outer + b) * 2 + c, (to_a * outer + (b + step) % outer) * 2 + to_c))
        return pairs

    def along_y(block, turn):
        return lax.ppermute(block, "y", [(i, (i + turn) % y_count) for i in range(y_count)])

    def columns(head):
        at = head * HD
        return jnp.stack([lax.dynamic_slice(x, (0, at), (TOK, HD)) for x in (keys, values)])

    other = columns(2 * (1 - x_lo) + (1 - x_hi))
    own = columns(2 * x_lo + x_hi)
    other = lax.ppermute(other, names, route(1, lambda a, c: (1 - a, 1 - c)))
    own = lax.ppermute(own, names, route(1, lambda a, c: (a, c)))

    message = pl.pallas_call(
        pack_queries,
        out_shape=shape(4, 2 * ROWS + AUX, HD),
        in_specs=[HBM] * 4,
        out_specs=HBM,
        scratch_shapes=[pltpu.VMEM((TOK, 2 * KVH * HD), bf16)] * 3
        + [
            pltpu.VMEM((2 * KVH, TOK), f32),
            pltpu.VMEM((4, 2 * ROWS + AUX, HD), bf16),
            pltpu.SemaphoreType.DMA((4,)),
            pltpu.SemaphoreType.DMA((4,)),
        ],
        compiler_params=WIDE,
        name="pack_queries",
    )(queries, attn_out, grad_out, row_total)
    own, message = lax.optimization_barrier((own, message))
    message = lax.all_to_all(message, ("x_hi", "x_lo"), 0, 0, tiled=True)

    kv = jnp.stack([other, own])
    stored = block_ids.reshape(y_count, 2, outer, 2)
    query_ids = lax.dynamic_slice(stored, (y, 0, o, 0), (1, 2, 1, 2)).reshape(2, 2)
    key_ids = lax.dynamic_slice(stored, (0, 0, (o + outer - 1) % outer, 0), (y_count, 2, 1, 2)).reshape(y_count, 2, 2)
    key_ids = jnp.concatenate([key_ids[::-1]] * 2)
    key_ids = lax.dynamic_slice(key_ids, (y_count - 1 - y, 0, 0), (y_count, 2, 2))
    key_ids = jnp.where(x_hi == 0, key_ids[:, ::-1], key_ids).reshape(y_count, 4, 1, 1)
    visible = key_ids < jnp.repeat(query_ids, 2, axis=0).reshape(1, 1, 4, 2)
    hide = jnp.repeat(jnp.where(visible, f32(0.0), f32(HIDDEN)), TOK, axis=3)

    turns = (1, 2, 3)
    blocks = [along_y(kv, turn) for turn in turns] + [kv]
    dq = None
    parts = []
    for turn, block in zip(turns + (0,), blocks):
        first, last = turn == turns[0], turn == 0
        dq, dkv = pl.pallas_call(
            functools.partial(attend, turn, first, last),
            out_shape=(
                shape(4, HD, ROWS) if last else jax.ShapeDtypeStruct((HD, 4 * ROWS), f32),
                jax.ShapeDtypeStruct((2, 2, TOK, HD), f32 if last else bf16),
            ),
            in_specs=[VMEM] * (3 if first else 4),
            out_specs=(VMEM, VMEM),
            compiler_params=PARAMS,
            scratch_shapes=[pltpu.VMEM((5, 4, ROWS), f32)],
            cost_estimate=LONG,
            name="attend_%d" % turn,
        )(hide, message, block, *(() if first else (dq,)))
        parts.append(dkv)
    def along_cores(block, step):
        axes = ("y", "outer")
        pairs = []
        for a in range(y_count):
            for b in range(outer):
                to_a, to_b = (a, b + 1) if b % 2 == 0 else ((a + 1) % y_count, b - 1)
                pair = (a * outer + b, to_a * outer + to_b)
                pairs.append(pair if step == 1 else pair[::-1])
        return lax.ppermute(block, axes, pairs)

    before, opposite, after, mine = parts
    before = along_cores(before, -1)
    after = along_cores(after, 1)
    opposite = along_y(opposite, 2)
    before, after, dq = lax.optimization_barrier((before, after, dq))
    before = along_cores(before, -1)
    after = along_cores(after, 1)
    dq = lax.all_to_all(dq, ("x_hi", "x_lo"), 0, 0, tiled=True)
    other, own = pl.pallas_call(
        add_partials,
        out_shape=(shape(2, TOK, HD), shape(2, TOK, HD)),
        in_specs=[VMEM] * 4,
        out_specs=(VMEM, VMEM),
        compiler_params=PARAMS,
        name="add_partials",
    )(mine, before, after, opposite)
    other = lax.ppermute(other, names, route(-1, lambda a, c: (1 - a, c)))
    own = lax.ppermute(own, names, route(-1, lambda a, c: (a, c)))
    grad_queries = pl.pallas_call(
        unpack_queries,
        out_shape=shape(TOK, 2 * KVH * HD),
        in_specs=[VMEM],
        out_specs=VMEM,
        compiler_params=PARAMS,
        name="unpack_queries",
    )(dq)
    grad_keys, grad_values = pl.pallas_call(
        unpack_kv,
        out_shape=(shape(TOK, 2 * HD), shape(TOK, 2 * HD)),
        in_specs=[VMEM] * 3,
        out_specs=(VMEM, VMEM),
        compiler_params=PARAMS,
        name="unpack_kv",
    )(jnp.full((8, HD), x_hi, jnp.int32), other, own)
    return grad_queries, grad_keys, grad_values


def solution(mesh):
    inner, outer, head = (mesh.shape[name] for name in ("inner", "outer", "head"))
    fine = Mesh(mesh.devices.reshape(inner // 2, 2, outer, head), ("y", "x_hi", "outer", "x_lo"))
    rows = ("y", "x_hi", "outer")
    in_specs = (
        P(rows, "x_lo"),
        P(rows, None),
        P(rows, None),
        P(rows, "x_lo"),
        P(rows, "x_lo"),
        P("x_lo", rows),
        P(),
    )
    out_specs = (P(rows, "x_lo"), P(rows, "x_lo"), P(rows, "x_lo"))
    return jax.shard_map(per_device, mesh=fine, in_specs=in_specs, out_specs=out_specs, check_vma=False)
```

```python
import functools
import math

import jax
import jax.numpy as jnp
from jax import lax
from jax.experimental import pallas as pl
from jax.experimental.pallas import tpu as pltpu
from jax.sharding import Mesh
from jax.sharding import PartitionSpec as P

KVH = 4
HD = 128
TOK = 256
HALF = 128
SCALE = 1.0 / math.sqrt(HD)
EXP2_SCALE = SCALE * math.log2(math.e)
HIDDEN = 1.0e30
ROWS = 2 * TOK
AUX = 32
NT = (((1,), (1,)), ((), ()))
NN = (((1,), (0,)), ((), ()))
VMEM = pl.BlockSpec(memory_space=pltpu.VMEM)
HBM = pl.BlockSpec(memory_space=pltpu.HBM)
SMEM = pl.BlockSpec(memory_space=pltpu.SMEM)
f32 = jnp.float32
bf16 = jnp.bfloat16
LONG = pl.CostEstimate(flops=2 * 10**10, bytes_accessed=0, transcendentals=0)
LONG = pl.CostEstimate(flops=10**10, bytes_accessed=0, transcendentals=0)
WIDE = pltpu.CompilerParams(vmem_limit_bytes=60 * 2**20)
PARAMS = pltpu.CompilerParams(vmem_limit_bytes=24 * 2**20)


def dot(a, b, dims):
    return lax.dot_general(a, b, dims, preferred_element_type=f32)


def split3(x):
    a = x.astype(bf16)
    r = x - a.astype(f32)
    b = r.astype(bf16)
    c = (r - b.astype(f32)).astype(bf16)
    return a, b, c


def head_of(x):
    return 2 * (x % 2) + x // 2


def pack_queries(queries, attn_out, grad_out, row_total, message, q_in, o_in, g_in, t_in, staged, sems, out_sems):
    copies = [
        pltpu.make_async_copy(source, target, sems.at[i])
        for i, (source, target) in enumerate(((row_total, t_in), (grad_out, g_in), (attn_out, o_in), (queries, q_in)))
    ]
    for copy in copies:
        copy.start()
    ones = jnp.ones((8, HD), bf16)
    copies[0].wait()
    log_total = jnp.log(t_in[...]) * f32(math.log2(math.e))
    copies[1].wait()
    copies[2].wait()
    sends = []
    for x in range(4):
        parts = []
        for n in range(2):
            h = n * KVH + head_of(x)
            columns = slice(h * HD, (h + 1) * HD)
            grad = g_in[:, columns]
            product = grad.astype(f32) * o_in[:, columns].astype(f32)
            high = product.astype(bf16)
            low = (product - high.astype(f32)).astype(bf16)
            delta = (dot(ones, high, NT) + dot(ones, low, NT))[0:1]
            parts.append((log_total[h : h + 1], delta))
            for half in range(2):
                at = ROWS + (half * 2 + n) * HALF
                staged[x, at : at + HALF] = grad[half * HALF : (half + 1) * HALF]
        table = []
        for which in range(2):
            for half in range(2):
                for n in range(2):
                    table.append(parts[n][which][:, half * HALF : (half + 1) * HALF])
        table = jnp.concatenate(table, axis=0)
        a, b, c = split3(table)
        pad = jnp.zeros((8, HALF), bf16)
        staged[x, 2 * ROWS : 2 * ROWS + AUX] = jnp.concatenate([a, b, c, pad], axis=0)
        if x == 0:
            copies[3].wait()
        for n in range(2):
            h = n * KVH + head_of(x)
            for half in range(2):
                at = (half * 2 + n) * HALF
                staged[x, at : at + HALF] = q_in[half * HALF : (half + 1) * HALF, h * HD : (h + 1) * HD]
        sends.append(pltpu.make_async_copy(staged.at[x], message.at[x], out_sems.at[x]))
        sends[-1].start()
    for send in sends:
        send.wait()


def attend(turn, first, last, *refs):
    hide, message, kv = refs[:3]
    dq_in = None if first else refs[3]
    dq_out, dkv, rows = refs[-3:]
    k = kv[:, 0].reshape(2 * TOK, HD)
    v = kv[:, 1].reshape(2 * TOK, HD)
    kt = k.T
    for x in range(4):
        table = message[x, 2 * ROWS : 2 * ROWS + AUX, :].astype(f32)
        table = table[0:8] + table[8:16] + table[16:24]
        for c in range(4):
            lanes = slice(c * HALF, (c + 1) * HALF)
            for i in range(4):
                rows[i, x : x + 1, lanes] = table[c : c + 1] + hide[turn, i, x : x + 1, lanes]
            rows[4, x : x + 1, lanes] = table[4 + c : 5 + c]
    dk = dv = None
    for x in range(4):
        q = message[x, 0:ROWS, :]
        g = message[x, ROWS : 2 * ROWS, :]
        scores = dot(k, q, NT)
        dprob = dot(v, g, NT)
        prob = jnp.concatenate(
            [
                jnp.exp2(scores[i * HALF : (i + 1) * HALF] * EXP2_SCALE - rows[i, x : x + 1, :])
                for i in range(4)
            ],
            axis=0,
        )
        ds = (prob * (dprob - rows[4, x : x + 1, :])).astype(bf16)
        dv_part = dot(prob.astype(bf16), g, NN)
        dk_part = dot(ds, q, NN)
        dv = dv_part if dv is None else dv + dv_part
        dk = dk_part if dk is None else dk + dk_part
        at = x * ROWS
        dq = dot(kt, ds, NN)
        if not first:
            dq = dq + dq_in[:, at : at + ROWS]
        if last:
            dq_out[x] = (dq * SCALE).astype(bf16)
        else:
            dq_out[:, at : at + ROWS] = dq
    dkv[:, 0] = (dk * SCALE).astype(dkv.dtype).reshape(2, TOK, HD)
    dkv[:, 1] = dv.astype(dkv.dtype).reshape(2, TOK, HD)


def add_partials(mine, a, b, c, other, own):
    for j, out in ((0, other), (1, own)):
        for i in range(2):
            out[i] = (a[j, i].astype(f32) + b[j, i].astype(f32) + c[j, i].astype(f32) + mine[j, i]).astype(bf16)


def unpack_queries(dq, grad_queries):
    for x in range(4):
        part = dq[x].T
        for n in range(2):
            h = n * KVH + head_of(x)
            for half in range(2):
                at = (half * 2 + n) * HALF
                grad_queries[half * HALF : (half + 1) * HALF, h * HD : (h + 1) * HD] = part[at : at + HALF]


def unpack_kv(swap, other, own, grad_keys, grad_values):
    second = swap[0:1, :] > 0
    for i, out in ((0, grad_keys), (1, grad_values)):
        out[:, 0:HD] = jnp.where(second, other[i], own[i])
        out[:, HD : 2 * HD] = jnp.where(second, own[i], other[i])


def shape(*dims):
    return jax.ShapeDtypeStruct(dims, bf16)


def per_device(queries, keys, values, attn_out, grad_out, row_total, block_ids):
    y_count = lax.axis_size("y")
    outer = lax.axis_size("outer")
    y = lax.axis_index("y")
    x_hi = lax.axis_index("x_hi")
    o = lax.axis_index("outer")
    x_lo = lax.axis_index("x_lo")
    names = ("x_hi", "outer", "x_lo")

    def route(step, turn):
        pairs = []
        for a in range(2):
            for b in range(outer):
                for c in range(2):
                    to_a, to_c = turn(a, c)
                    pairs.append(((a * outer + b) * 2 + c, (to_a * outer + (b + step) % outer) * 2 + to_c))
        return pairs

    def along_y(block, turn):
        return lax.ppermute(block, "y", [(i, (i + turn) % y_count) for i in range(y_count)])

    def columns(head):
        at = head * HD
        return jnp.stack([lax.dynamic_slice(x, (0, at), (TOK, HD)) for x in (keys, values)])

    other = columns(2 * (1 - x_lo) + (1 - x_hi))
    own = columns(2 * x_lo + x_hi)
    other = lax.ppermute(other, names, route(1, lambda a, c: (1 - a, 1 - c)))
    own = lax.ppermute(own, names, route(1, lambda a, c: (a, c)))

    message = pl.pallas_call(
        pack_queries,
        out_shape=shape(4, 2 * ROWS + AUX, HD),
        in_specs=[HBM] * 4,
        out_specs=HBM,
        scratch_shapes=[pltpu.VMEM((TOK, 2 * KVH * HD), bf16)] * 3
        + [
            pltpu.VMEM((2 * KVH, TOK), f32),
            pltpu.VMEM((4, 2 * ROWS + AUX, HD), bf16),
            pltpu.SemaphoreType.DMA((4,)),
            pltpu.SemaphoreType.DMA((4,)),
        ],
        compiler_params=WIDE,
        name="pack_queries",
    )(queries, attn_out, grad_out, row_total)
    own, message = lax.optimization_barrier((own, message))
    message = lax.all_to_all(message, ("x_hi", "x_lo"), 0, 0, tiled=True)

    kv = jnp.stack([other, own])
    stored = block_ids.reshape(y_count, 2, outer, 2)
    query_ids = lax.dynamic_slice(stored, (y, 0, o, 0), (1, 2, 1, 2)).reshape(2, 2)
    key_ids = lax.dynamic_slice(stored, (0, 0, (o + outer - 1) % outer, 0), (y_count, 2, 1, 2)).reshape(y_count, 2, 2)
    key_ids = jnp.concatenate([key_ids[::-1]] * 2)
    key_ids = lax.dynamic_slice(key_ids, (y_count - 1 - y, 0, 0), (y_count, 2, 2))
    key_ids = jnp.where(x_hi == 0, key_ids[:, ::-1], key_ids).reshape(y_count, 4, 1, 1)
    visible = key_ids < jnp.repeat(query_ids, 2, axis=0).reshape(1, 1, 4, 2)
    hide = jnp.repeat(jnp.where(visible, f32(0.0), f32(HIDDEN)), TOK, axis=3)

    turns = (1, 3, 2)
    blocks = [along_y(kv, turn) for turn in turns] + [kv]
    dq = None
    parts = []
    for turn, block in zip(turns + (0,), blocks):
        first, last = turn == turns[0], turn == 0
        dq, dkv = pl.pallas_call(
            functools.partial(attend, turn, first, last),
            out_shape=(
                shape(4, HD, ROWS) if last else jax.ShapeDtypeStruct((HD, 4 * ROWS), f32),
                jax.ShapeDtypeStruct((2, 2, TOK, HD), f32 if last else bf16),
            ),
            in_specs=[VMEM] * (3 if first else 4),
            out_specs=(VMEM, VMEM),
            compiler_params=PARAMS,
            scratch_shapes=[pltpu.VMEM((5, 4, ROWS), f32)],
            cost_estimate=LONG,
            name="attend_%d" % turn,
        )(hide, message, block, *(() if first else (dq,)))
        parts.append(dkv)
    def along_cores(block, step):
        axes = ("y", "outer")
        pairs = []
        for a in range(y_count):
            for b in range(outer):
                to_a, to_b = (a, b + 1) if b % 2 == 0 else ((a + 1) % y_count, b - 1)
                pair = (a * outer + b, to_a * outer + to_b)
                pairs.append(pair if step == 1 else pair[::-1])
        return lax.ppermute(block, axes, pairs)

    before, after, opposite, mine = parts
    before = along_cores(before, -1)
    after = along_cores(after, 1)
    opposite = along_y(opposite, 2)
    before, after, dq = lax.optimization_barrier((before, after, dq))
    before = along_cores(before, -1)
    after = along_cores(after, 1)
    dq = lax.all_to_all(dq, ("x_hi", "x_lo"), 0, 0, tiled=True)
    other, own = pl.pallas_call(
        add_partials,
        out_shape=(shape(2, TOK, HD), shape(2, TOK, HD)),
        in_specs=[VMEM] * 4,
        out_specs=(VMEM, VMEM),
        compiler_params=PARAMS,
        name="add_partials",
    )(mine, before, after, opposite)
    other = lax.ppermute(other, names, route(-1, lambda a, c: (1 - a, c)))
    own = lax.ppermute(own, names, route(-1, lambda a, c: (a, c)))
    grad_queries = pl.pallas_call(
        unpack_queries,
        out_shape=shape(TOK, 2 * KVH * HD),
        in_specs=[VMEM],
        out_specs=VMEM,
        compiler_params=PARAMS,
        name="unpack_queries",
    )(dq)
    grad_keys, grad_values = pl.pallas_call(
        unpack_kv,
        out_shape=(shape(TOK, 2 * HD), shape(TOK, 2 * HD)),
        in_specs=[VMEM] * 3,
        out_specs=(VMEM, VMEM),
        compiler_params=PARAMS,
        name="unpack_kv",
    )(jnp.full((8, HD), x_hi, jnp.int32), other, own)
    return grad_queries, grad_keys, grad_values


def solution(mesh):
    inner, outer, head = (mesh.shape[name] for name in ("inner", "outer", "head"))
    fine = Mesh(mesh.devices.reshape(inner // 2, 2, outer, head), ("y", "x_hi", "outer", "x_lo"))
    rows = ("y", "x_hi", "outer")
    in_specs = (
        P(rows, "x_lo"),
        P(rows, None),
        P(rows, None),
        P(rows, "x_lo"),
        P(rows, "x_lo"),
        P("x_lo", rows),
        P(),
    )
    out_specs = (P(rows, "x_lo"), P(rows, "x_lo"), P(rows, "x_lo"))
    return jax.shard_map(per_device, mesh=fine, in_specs=in_specs, out_specs=out_specs, check_vma=False)
```

```python
import functools
import math

import jax
import jax.numpy as jnp
from jax import lax
from jax.experimental import pallas as pl
from jax.experimental.pallas import tpu as pltpu
from jax.sharding import Mesh
from jax.sharding import PartitionSpec as P

KVH = 4
HD = 128
TOK = 256
HALF = 128
SCALE = 1.0 / math.sqrt(HD)
EXP2_SCALE = SCALE * math.log2(math.e)
HIDDEN = 1.0e30
ROWS = 2 * TOK
AUX = 32
NT = (((1,), (1,)), ((), ()))
NN = (((1,), (0,)), ((), ()))
VMEM = pl.BlockSpec(memory_space=pltpu.VMEM)
HBM = pl.BlockSpec(memory_space=pltpu.HBM)
SMEM = pl.BlockSpec(memory_space=pltpu.SMEM)
f32 = jnp.float32
bf16 = jnp.bfloat16
LONG = pl.CostEstimate(flops=2 * 10**10, bytes_accessed=0, transcendentals=0)
LONG = pl.CostEstimate(flops=10**10, bytes_accessed=0, transcendentals=0)
WIDE = pltpu.CompilerParams(vmem_limit_bytes=60 * 2**20)
PARAMS = pltpu.CompilerParams(vmem_limit_bytes=24 * 2**20)


def dot(a, b, dims):
    return lax.dot_general(a, b, dims, preferred_element_type=f32)


def split3(x):
    a = x.astype(bf16)
    r = x - a.astype(f32)
    b = r.astype(bf16)
    c = (r - b.astype(f32)).astype(bf16)
    return a, b, c


def head_of(x):
    return 2 * (x % 2) + x // 2


def pack_queries(queries, attn_out, grad_out, row_total, message, q_in, o_in, g_in, t_in, staged, sems, out_sems):
    copies = [
        pltpu.make_async_copy(source, target, sems.at[i])
        for i, (source, target) in enumerate(((row_total, t_in), (grad_out, g_in), (attn_out, o_in), (queries, q_in)))
    ]
    for copy in copies:
        copy.start()
    ones = jnp.ones((8, HD), bf16)
    copies[0].wait()
    log_total = jnp.log(t_in[...]) * f32(math.log2(math.e))
    copies[1].wait()
    copies[2].wait()
    sends = []
    for x in range(4):
        parts = []
        for n in range(2):
            h = n * KVH + head_of(x)
            columns = slice(h * HD, (h + 1) * HD)
            grad = g_in[:, columns]
            product = grad.astype(f32) * o_in[:, columns].astype(f32)
            high = product.astype(bf16)
            low = (product - high.astype(f32)).astype(bf16)
            delta = (dot(ones, high, NT) + dot(ones, low, NT))[0:1]
            parts.append((log_total[h : h + 1], delta))
            for half in range(2):
                at = ROWS + (half * 2 + n) * HALF
                staged[x, at : at + HALF] = grad[half * HALF : (half + 1) * HALF]
        table = []
        for which in range(2):
            for half in range(2):
                for n in range(2):
                    table.append(parts[n][which][:, half * HALF : (half + 1) * HALF])
        table = jnp.concatenate(table, axis=0)
        a, b, c = split3(table)
        pad = jnp.zeros((8, HALF), bf16)
        staged[x, 2 * ROWS : 2 * ROWS + AUX] = jnp.concatenate([a, b, c, pad], axis=0)
        if x == 0:
            copies[3].wait()
        for n in range(2):
            h = n * KVH + head_of(x)
            for half in range(2):
                at = (half * 2 + n) * HALF
                staged[x, at : at + HALF] = q_in[half * HALF : (half + 1) * HALF, h * HD : (h + 1) * HD]
        sends.append(pltpu.make_async_copy(staged.at[x], message.at[x], out_sems.at[x]))
        sends[-1].start()
    for send in sends:
        send.wait()


def attend(turn, first, last, *refs):
    hide, message, kv = refs[:3]
    dq_in = None if first else refs[3]
    dq_out, dkv, rows = refs[-3:]
    k = kv[:, 0].reshape(2 * TOK, HD)
    v = kv[:, 1].reshape(2 * TOK, HD)
    kt = k.T
    for x in range(4):
        table = message[x, 2 * ROWS : 2 * ROWS + AUX, :].astype(f32)
        table = table[0:8] + table[8:16] + table[16:24]
        for c in range(4):
            lanes = slice(c * HALF, (c + 1) * HALF)
            for i in range(4):
                rows[i, x : x + 1, lanes] = table[c : c + 1] + hide[turn, i, x : x + 1, lanes]
            rows[4, x : x + 1, lanes] = table[4 + c : 5 + c]
    dk = dv = None
    for x in range(4):
        q = message[x, 0:ROWS, :]
        g = message[x, ROWS : 2 * ROWS, :]
        scores = dot(k, q, NT)
        dprob = dot(v, g, NT)
        prob = jnp.concatenate(
            [
                jnp.exp2(scores[i * HALF : (i + 1) * HALF] * EXP2_SCALE - rows[i, x : x + 1, :])
                for i in range(4)
            ],
            axis=0,
        )
        ds = (prob * (dprob - rows[4, x : x + 1, :])).astype(bf16)
        dv_part = dot(prob.astype(bf16), g, NN)
        dk_part = dot(ds, q, NN)
        dv = dv_part if dv is None else dv + dv_part
        dk = dk_part if dk is None else dk + dk_part
        at = x * ROWS
        dq = dot(kt, ds, NN)
        if not first:
            dq = dq + dq_in[:, at : at + ROWS]
        if last:
            dq_out[x] = (dq * SCALE).astype(bf16)
        else:
            dq_out[:, at : at + ROWS] = dq
    dkv[:, 0] = (dk * SCALE).astype(dkv.dtype).reshape(2, TOK, HD)
    dkv[:, 1] = dv.astype(dkv.dtype).reshape(2, TOK, HD)


def add_partials(mine, a, b, c, other, own):
    for j, out in ((0, other), (1, own)):
        for i in range(2):
            out[i] = (a[j, i].astype(f32) + b[j, i].astype(f32) + c[j, i].astype(f32) + mine[j, i]).astype(bf16)


def unpack_queries(dq, grad_queries):
    for x in range(4):
        part = dq[x].T
        for n in range(2):
            h = n * KVH + head_of(x)
            for half in range(2):
                at = (half * 2 + n) * HALF
                grad_queries[half * HALF : (half + 1) * HALF, h * HD : (h + 1) * HD] = part[at : at + HALF]


def unpack_kv(swap, other, own, grad_keys, grad_values):
    second = swap[0:1, :] > 0
    for i, out in ((0, grad_keys), (1, grad_values)):
        out[:, 0:HD] = jnp.where(second, other[i], own[i])
        out[:, HD : 2 * HD] = jnp.where(second, own[i], other[i])


def shape(*dims):
    return jax.ShapeDtypeStruct(dims, bf16)


def per_device(queries, keys, values, attn_out, grad_out, row_total, block_ids):
    y_count = lax.axis_size("y")
    outer = lax.axis_size("outer")
    y = lax.axis_index("y")
    x_hi = lax.axis_index("x_hi")
    o = lax.axis_index("outer")
    x_lo = lax.axis_index("x_lo")
    names = ("x_hi", "outer", "x_lo")

    def route(step, turn):
        pairs = []
        for a in range(2):
            for b in range(outer):
                for c in range(2):
                    to_a, to_c = turn(a, c)
                    pairs.append(((a * outer + b) * 2 + c, (to_a * outer + (b + step) % outer) * 2 + to_c))
        return pairs

    def along_y(block, turn):
        return lax.ppermute(block, "y", [(i, (i + turn) % y_count) for i in range(y_count)])

    def columns(head):
        at = head * HD
        return jnp.stack([lax.dynamic_slice(x, (0, at), (TOK, HD)) for x in (keys, values)])

    other = columns(2 * (1 - x_lo) + (1 - x_hi))
    own = columns(2 * x_lo + x_hi)
    other = lax.ppermute(other, names, route(1, lambda a, c: (1 - a, 1 - c)))
    own = lax.ppermute(own, names, route(1, lambda a, c: (a, c)))

    message = pl.pallas_call(
        pack_queries,
        out_shape=shape(4, 2 * ROWS + AUX, HD),
        in_specs=[HBM] * 4,
        out_specs=HBM,
        scratch_shapes=[pltpu.VMEM((TOK, 2 * KVH * HD), bf16)] * 3
        + [
            pltpu.VMEM((2 * KVH, TOK), f32),
            pltpu.VMEM((4, 2 * ROWS + AUX, HD), bf16),
            pltpu.SemaphoreType.DMA((4,)),
            pltpu.SemaphoreType.DMA((4,)),
        ],
        compiler_params=WIDE,
        name="pack_queries",
    )(queries, attn_out, grad_out, row_total)
    own, message = lax.optimization_barrier((own, message))
    message = lax.all_to_all(message, ("x_hi", "x_lo"), 0, 0, tiled=True)

    kv = jnp.stack([other, own])
    stored = block_ids.reshape(y_count, 2, outer, 2)
    query_ids = lax.dynamic_slice(stored, (y, 0, o, 0), (1, 2, 1, 2)).reshape(2, 2)
    key_ids = lax.dynamic_slice(stored, (0, 0, (o + outer - 1) % outer, 0), (y_count, 2, 1, 2)).reshape(y_count, 2, 2)
    key_ids = jnp.concatenate([key_ids[::-1]] * 2)
    key_ids = lax.dynamic_slice(key_ids, (y_count - 1 - y, 0, 0), (y_count, 2, 2))
    key_ids = jnp.where(x_hi == 0, key_ids[:, ::-1], key_ids).reshape(y_count, 4, 1, 1)
    visible = key_ids < jnp.repeat(query_ids, 2, axis=0).reshape(1, 1, 4, 2)
    hide = jnp.repeat(jnp.where(visible, f32(0.0), f32(HIDDEN)), TOK, axis=3)

    turns = (1, 3, 2)
    blocks = [along_y(kv, turn) for turn in turns] + [kv]
    dq = None
    parts = []
    for turn, block in zip(turns + (0,), blocks):
        first, last = turn == turns[0], turn == 0
        dq, dkv = pl.pallas_call(
            functools.partial(attend, turn, first, last),
            out_shape=(
                shape(4, HD, ROWS) if last else jax.ShapeDtypeStruct((HD, 4 * ROWS), f32),
                jax.ShapeDtypeStruct((2, 2, TOK, HD), f32 if last else bf16),
            ),
            in_specs=[VMEM] * (3 if first else 4),
            out_specs=(VMEM, VMEM),
            compiler_params=PARAMS,
            scratch_shapes=[pltpu.VMEM((5, 4, ROWS), f32)],
            cost_estimate=LONG,
            name="attend_%d" % turn,
        )(hide, message, block, *(() if first else (dq,)))
        parts.append(dkv)
    def along_cores(block, step):
        axes = ("y", "outer")
        pairs = []
        for a in range(y_count):
            for b in range(outer):
                to_a, to_b = (a, b + 1) if b % 2 == 0 else ((a + 1) % y_count, b - 1)
                pair = (a * outer + b, to_a * outer + to_b)
                pairs.append(pair if step == 1 else pair[::-1])
        return lax.ppermute(block, axes, pairs)

    before, after, opposite, mine = parts
    before = along_cores(before, -1)
    after = along_cores(after, 1)
    opposite = along_y(opposite, 2)
    before = along_cores(before, -1)
    after, dq = lax.optimization_barrier((after, dq))
    after = along_cores(after, 1)
    dq = lax.all_to_all(dq, ("x_hi", "x_lo"), 0, 0, tiled=True)
    other, own = pl.pallas_call(
        add_partials,
        out_shape=(shape(2, TOK, HD), shape(2, TOK, HD)),
        in_specs=[VMEM] * 4,
        out_specs=(VMEM, VMEM),
        compiler_params=PARAMS,
        name="add_partials",
    )(mine, before, after, opposite)
    other = lax.ppermute(other, names, route(-1, lambda a, c: (1 - a, c)))
    own = lax.ppermute(own, names, route(-1, lambda a, c: (a, c)))
    grad_queries = pl.pallas_call(
        unpack_queries,
        out_shape=shape(TOK, 2 * KVH * HD),
        in_specs=[VMEM],
        out_specs=VMEM,
        compiler_params=PARAMS,
        name="unpack_queries",
    )(dq)
    grad_keys, grad_values = pl.pallas_call(
        unpack_kv,
        out_shape=(shape(TOK, 2 * HD), shape(TOK, 2 * HD)),
        in_specs=[VMEM] * 3,
        out_specs=(VMEM, VMEM),
        compiler_params=PARAMS,
        name="unpack_kv",
    )(jnp.full((8, HD), x_hi, jnp.int32), other, own)
    return grad_queries, grad_keys, grad_values


def solution(mesh):
    inner, outer, head = (mesh.shape[name] for name in ("inner", "outer", "head"))
    fine = Mesh(mesh.devices.reshape(inner // 2, 2, outer, head), ("y", "x_hi", "outer", "x_lo"))
    rows = ("y", "x_hi", "outer")
    in_specs = (
        P(rows, "x_lo"),
        P(rows, None),
        P(rows, None),
        P(rows, "x_lo"),
        P(rows, "x_lo"),
        P("x_lo", rows),
        P(),
    )
    out_specs = (P(rows, "x_lo"), P(rows, "x_lo"), P(rows, "x_lo"))
    return jax.shard_map(per_device, mesh=fine, in_specs=in_specs, out_specs=out_specs, check_vma=False)
```
